32 devices in a mesh: ctx: 16 (over z, x, core), dp: 2 (over y).
Axes of the slice: x: 2, y: 2, z: 4, core: 2. Of those that a mesh axis runs over, the one named last changes fastest.
Arguments:
- hidden_in: bfloat16 [2048, 2048], P('ctx'), may hold values from -6 to 6
- query_vectors: bfloat16 [2048, 1024], P('ctx', 'dp'), may hold values from -6 to 6
- key_vectors: bfloat16 [2048, 1024], P('ctx', 'dp')
- value_vectors: bfloat16 [2048, 2048], P('ctx', 'dp'), may hold values from -6 to 6
- out_cotangent: bfloat16 [2048, 2048], P('ctx', 'dp'), may hold values from -6 to 6
- w_decay: bfloat16 [2048, 16], P(None, 'dp'), may hold values from -0.125 to 0.125
- w_beta: bfloat16 [2048, 16], P(None, 'dp'), may hold values from -0.125 to 0.125
- log_decay_rate: float32 [16], P('dp')
- step_bias: float32 [16], P('dp'), may hold values from -1 to 1
- doc_start: int32 [1], replicated, may hold values from 0 to 2047
Outputs:
- query_grad: bfloat16 [2048, 1024], P('ctx', 'dp')
- key_grad: bfloat16 [2048, 1024], P('ctx', 'dp')
- value_grad: bfloat16 [2048, 2048], P('ctx', 'dp')
- hidden_grad: bfloat16 [2048, 2048], P('ctx', 'dp')
- w_decay_grad: float32 [2048, 16], P(None, 'dp')
- w_beta_grad: float32 [2048, 16], P(None, 'dp')
- rate_grad: float32 [16], P('dp')
- bias_grad: float32 [16], P('dp')
The draws below stay inside these ranges and needn't reach their ends.
Inputs may be any that keep to these rules, and one draw needn't show every extreme that they name: `doc_start`: the state is cleared at that position.
All inputs are finite; a program needn't handle non-finite values.
Results may differ from the reference program's by a relative error of at most 0.0024.
Values may be sent and summed in bfloat16 or wider, within the bound.
A program may use at most 128 MiB of HBM per device.

```python
import jax
import jax.numpy as jnp
from jax import lax

D = 2048
HV = 16
HK = 8
DK = 128
DV = 128
BLOCK = 64
TOKENS = 2048


def draw_key_vectors(key, part):
    key = jax.random.fold_in(key, 11)
    direction_key, loading_key, jitter_key = jax.random.split(key, 3)
    jitter_level = (8.0 * DK / TOKENS) ** 0.5
    directions = jax.random.normal(direction_key, (4, HK, DK), jnp.float32)
    loadings = jax.random.normal(loading_key, (4, TOKENS, HK, 1), jnp.float32)
    jitter = jax.random.normal(jitter_key, (TOKENS, HK, DK), jnp.float32)
    shared = loadings[0] * directions[0]
    for position in range(1, 4):
        shared = shared + loadings[position] * directions[position]
    blended = shared + jitter_level * jitter
    return blended.reshape(TOKENS, HK * DK).astype(jnp.bfloat16)


def draw_log_decay_rate(key, part):
    key = jax.random.fold_in(key, 23)
    chooser_key, slow_key, fast_key = jax.random.split(key, 3)
    slow_share = 0.5
    slow_scale = jnp.exp(jax.random.uniform(slow_key, (HV,), jnp.float32, jnp.log(0.1), jnp.log(1.5)))
    chooser = jax.random.uniform(chooser_key, (HV,), jnp.float32)
    slow_rates = jnp.log(slow_scale / TOKENS)
    fast_rates = jax.random.uniform(fast_key, (HV,), jnp.float32, -3.6, -3.0)
    return jnp.where(chooser < slow_share, slow_rates, fast_rates).astype(jnp.float32)


def shard_levels(rng, extent, cuts, least, top_value):
    def one(dim, blocks):
        steps = jax.random.uniform(jax.random.fold_in(jax.random.fold_in(rng, 6), dim), (blocks,), jnp.float32, least / len(cuts), top_value / len(cuts))
        return jnp.repeat(jnp.exp(steps), extent[dim] // blocks).reshape((-1,) + (1,) * (len(extent) - dim - 1))

    loudness = one(*cuts[0])
    for cut in cuts[1:]:
        loudness = loudness * one(*cut)
    return loudness


def centred(key, shape, scale, bound, cuts=(), kind=jnp.bfloat16):
    entries = jax.random.normal(key, shape, jnp.float32) * scale
    if len(cuts) > 0:
        entries = shard_levels(key, shape, cuts, -0.22, 0.18) * entries
    return jnp.clip(entries, min=-bound, max=bound).astype(kind)


def setup_inputs(seed: int = 0) -> dict:
    keys = jax.random.split(jax.random.key(seed), 11)
    hidden_in = centred(keys[0], (TOKENS, D), 1.0, 6.0, ((0, 16),))
    query_vectors = centred(keys[1], (TOKENS, HK * DK), 1.0, 6.0, ((0, 16), (1, 2)))
    key_vectors = draw_key_vectors(jax.random.fold_in(keys[10], 71), 0)
    value_vectors = centred(keys[3], (TOKENS, HV * DV), 1.0, 6.0, ((0, 16), (1, 2)))
    out_cotangent = centred(keys[4], (TOKENS, HV * DV), 1.0, 6.0, ((0, 16), (1, 2)))
    w_decay = centred(keys[5], (D, HV), D ** -0.5, 0.125, ((1, 2),))
    w_beta = centred(keys[6], (D, HV), D ** -0.5, 0.125, ((1, 2),))
    log_decay_rate = draw_log_decay_rate(jax.random.fold_in(keys[10], 71), 0)
    step_bias = jnp.clip(jax.random.uniform(keys[8], (HV,), jnp.float32, -1.0, 1.0) * shard_levels(keys[8], (HV,), ((0, 2),), -0.4, 0.0), -1.0, 1.0)
    doc_start = jax.random.randint(keys[9], (1,), 0, TOKENS).astype(jnp.int32)
    return {"hidden_in": hidden_in, "query_vectors": query_vectors, "key_vectors": key_vectors, "value_vectors": value_vectors, "out_cotangent": out_cotangent, "w_decay": w_decay, "w_beta": w_beta, "log_decay_rate": log_decay_rate, "step_bias": step_bias, "doc_start": doc_start}


norm_epsilon = 1e-06

def unit_rows(source):
    return source * lax.rsqrt(lax.optimization_barrier(jnp.sum(source * source, axis=-1, keepdims=True)) + norm_epsilon)

def block_step(carried, pieces):
    query_block, key_block, value_block, decay_block, beta_block, reset_block = pieces
    length = query_block.shape[-2]
    highest = lax.Precision.HIGHEST
    cumulative = jnp.cumsum(decay_block, axis=-1)
    counted = jnp.cumsum(reset_block, axis=-1)
    places = jnp.arange(length, dtype=jnp.int32)
    lower_mask = places[:, None] >= places[None, :]
    strict_mask = places[:, None] > places[None, :]
    same_doc = (counted[:, :, None] == counted[:, None, :])[:, None]
    keep_mask = jnp.logical_and(lower_mask, same_doc)
    spread = cumulative[..., :, None] - cumulative[..., None, :]
    decay_matrix = jnp.where(keep_mask, jnp.exp(jnp.where(keep_mask, spread, 0.0)), 0.0)
    carry_in = jnp.where(counted[:, None, :] == 0, jnp.exp(cumulative), 0.0)
    key_gram = jnp.einsum('bhid,bhjd->bhij', key_block, key_block, precision=highest)
    coupling = jnp.where(strict_mask, beta_block[..., :, None] * decay_matrix * key_gram, 0.0)
    key_state = jnp.einsum('bhid,bhde->bhie', key_block, carried, precision=highest)
    target = beta_block[..., None] * (value_block - carry_in[..., None] * key_state)
    system = coupling + jnp.eye(length, dtype=jnp.float32)
    updates = lax.linalg.triangular_solve(system, target, left_side=True, lower=True, unit_diagonal=True)
    query_key = jnp.einsum('bhid,bhjd->bhij', query_block, key_block, precision=highest)
    from_state = jnp.einsum('bhid,bhde->bhie', query_block, carried, precision=highest)
    outputs = carry_in[..., None] * from_state + jnp.einsum('bhij,bhje->bhie', query_key * decay_matrix, updates, precision=highest)
    weighted_keys = key_block * decay_matrix[..., -1, :, None]
    new_state = carry_in[..., -1, None, None] * carried + jnp.einsum('bhjd,bhje->bhde', weighted_keys, updates, precision=highest)
    return (new_state, outputs)

def blocked(source, blocks):
    seq_count, tokens = (source.shape[0], source.shape[1])
    shaped = source.reshape((seq_count, blocks, tokens // blocks) + source.shape[2:])
    if source.ndim == 4:
        return shaped.transpose(1, 0, 3, 2, 4)
    if source.ndim == 3:
        return shaped.transpose(1, 0, 3, 2)
    return shaped.transpose(1, 0, 2)

def run_block(carried, queries_f, keys_f, values_f, logit_rows, rate_logs, biases, resets):
    seq_count, tokens = (logit_rows.shape[0], logit_rows.shape[1])
    head_count = rate_logs.shape[0]
    size_key = carried.shape[2]
    size_value = carried.shape[3]
    group_size = head_count // (queries_f.shape[2] // size_key)
    log_decay = -jnp.exp(rate_logs) * jax.nn.softplus(logit_rows[..., :head_count] + biases)
    beta_all = jax.nn.sigmoid(logit_rows[..., head_count:])
    query_heads = unit_rows(queries_f.reshape(seq_count, tokens, -1, size_key)) * size_key ** (-0.5)
    key_heads = unit_rows(keys_f.reshape(seq_count, tokens, -1, size_key))
    query_heads = jnp.repeat(query_heads, group_size, axis=2)
    key_heads = jnp.repeat(key_heads, group_size, axis=2)
    value_heads = values_f.reshape(seq_count, tokens, head_count, size_value)
    blocks = tokens // BLOCK
    pieces = (blocked(query_heads, blocks), blocked(key_heads, blocks), blocked(value_heads, blocks), blocked(log_decay, blocks), blocked(beta_all, blocks), blocked(resets, blocks))
    final_state, outputs = lax.scan(jax.checkpoint(block_step), carried, pieces)
    outputs = outputs.transpose(1, 0, 3, 2, 4).reshape(seq_count, tokens, head_count * size_value)
    return (outputs, final_state)

def reference(hidden_in, query_vectors, key_vectors, value_vectors, out_cotangent, w_decay, w_beta, log_decay_rate, step_bias, doc_start):
    both_weights = jnp.concatenate([w_decay, w_beta], axis=1)
    head_count = log_decay_rate.shape[0]
    positions = jnp.arange(TOKENS, dtype=jnp.int32)
    zero_state = jnp.zeros((1, head_count, DK, DV), jnp.float32)
    highest = lax.Precision.HIGHEST
    logits = jnp.dot(hidden_in.astype(jnp.float32), both_weights.astype(jnp.float32), preferred_element_type=jnp.float32)[None]
    resets = (positions == doc_start[0].astype(jnp.int32)).astype(jnp.float32)[None]

    def forward(queries_f, keys_f, values_f, logit_rows, rate_logs, biases):
        return run_block(zero_state, queries_f, keys_f, values_f, logit_rows, rate_logs, biases, resets)[0]
    result, pull_back = jax.vjp(forward, query_vectors.astype(jnp.float32)[None], key_vectors.astype(jnp.float32)[None], value_vectors.astype(jnp.float32)[None], logits, log_decay_rate, step_bias)
    gradients = pull_back(out_cotangent.astype(jnp.float32)[None])
    logit_grad = gradients[3][0]
    hidden_grad = jnp.dot(logit_grad, both_weights.astype(jnp.float32).T, precision=highest)
    weight_grad = jnp.dot(hidden_in.astype(jnp.float32).T, logit_grad, precision=highest)
    return (gradients[0][0].astype(jnp.bfloat16), gradients[1][0].astype(jnp.bfloat16), gradients[2][0].astype(jnp.bfloat16), hidden_grad.astype(jnp.bfloat16), weight_grad[:, :head_count], weight_grad[:, head_count:], gradients[4], gradients[5])
```

```python
import functools

import jax
import jax.numpy as jnp
from jax import lax
from jax.experimental import pallas as pl
from jax.experimental.pallas import tpu as pltpu
from jax.sharding import PartitionSpec as P

DK = 128
DV = 128
LANES = 128
norm_epsilon = 1e-06

MESH = pl.DeviceIdType.MESH
NN = ((1,), (0,))
NT = ((1,), (1,))
TN = ((0,), (0,))
f32 = jnp.float32
bf16 = jnp.bfloat16
VMEM_LIMIT = 56 * 1024 * 1024


def one_pass(a, b, dims):
    return lax.dot_general(a, b, (dims, ((), ())), preferred_element_type=f32)


def split(x):
    if isinstance(x, tuple):
        return x
    if x.dtype == bf16:
        return (x,)
    high = x.astype(bf16)
    return (high, (x - high.astype(f32)).astype(bf16))


def split3(x):
    high = x.astype(bf16)
    rest = x - high.astype(f32)
    middle = rest.astype(bf16)
    return (high, middle, (rest - middle.astype(f32)).astype(bf16))


def mm(a, b, dims=NN):
    a, b = split(a), split(b)
    total = None
    for i, left in enumerate(a):
        for j, right in enumerate(b):
            if i + j < max(len(a), len(b)):
                term = one_pass(left, right, dims)
                total = term if total is None else total + term
    return total


def iotas():
    rows = lax.broadcasted_iota(jnp.int32, (LANES, LANES), 0)
    columns = lax.broadcasted_iota(jnp.int32, (LANES, LANES), 1)
    return rows, columns


def as_row(eye, column):
    return jnp.sum(jnp.where(eye, column, 0.0), axis=0, keepdims=True)


def as_column(eye, row):
    return jnp.sum(jnp.where(eye, row, 0.0), axis=1, keepdims=True)


def rsum(x):
    return jnp.sum(x, axis=1, keepdims=True)


def gates(logits, rate_row, bias_row, heads):
    x = logits + bias_row
    softplus = jnp.maximum(x, 0.0) + jnp.log1p(jnp.exp(-jnp.abs(x)))
    return -jnp.exp(rate_row) * softplus


def sigmoid(x):
    return 1.0 / (1.0 + jnp.exp(-x))


def scales(raw):
    wide = raw.astype(f32)
    return lax.rsqrt(rsum(wide * wide) + norm_epsilon)


def head_slice(ref, index):
    return ref[:, index * 128 : (index + 1) * 128]


def segment(doc, offset, size):
    inside = jnp.logical_and(doc >= offset, doc < offset + size)
    place = jnp.where(inside, doc - offset, size)
    return place


def decay_parts(eye, lower, rows, columns, cum_col, place):
    cum_row = as_row(eye, cum_col)
    keep = jnp.logical_and(lower, (rows >= place) == (columns >= place))
    decay = jnp.where(keep, jnp.exp(jnp.where(keep, cum_col - cum_row, 0.0)), 0.0)
    places = rows[:, :1]
    carry = jnp.where(places < place, jnp.exp(cum_col), 0.0)
    last = cum_col[LANES - 1 : LANES, :]
    same = jnp.logical_or(places >= place, place >= LANES)
    to_last = jnp.where(same, jnp.exp(jnp.where(same, last - cum_col, 0.0)), 0.0)
    return decay, carry, to_last, carry[LANES - 1 : LANES, :]


def first_kernel(
    heads, place_ref, hid_ref, w_ref, q_ref, k_ref, v_ref, do_ref, rate_ref, bias_ref,
    a_ref, b_ref, n_ref, t_ref, w_out_ref, u_ref, p_ref, logit_ref, cum_ref,
):
    rows, columns = iotas()
    eye = rows == columns
    lower = rows >= columns
    strict = rows > columns
    place = place_ref[0]
    logits = one_pass(hid_ref[...], w_ref[...], NN)
    logit_ref[...] = logits
    log_decay = gates(logits, rate_ref[...], bias_ref[...], heads)
    ones = lower.astype(f32).astype(bf16)
    cum = mm(ones, split3(log_decay))
    cum_ref[...] = cum
    beta_all = sigmoid(logits)
    eye_f = eye.astype(f32)
    group = heads // (q_ref.shape[1] // DK)
    decays, betas, rks, rqs, couplings = [], [], [], [], []
    for h in range(heads):
        if h % group == 0:
            kb, qb = head_slice(k_ref, h // group), head_slice(q_ref, h // group)
            rk = scales(kb)
            rq = scales(qb) * DK ** (-0.5)
            rk_row = as_row(eye, rk)
            gram = one_pass(kb, kb, NT) * rk * rk_row
            query_key = one_pass(qb, kb, NT) * rq * rk_row
        parts = decay_parts(eye, lower, rows, columns, cum[:, h : h + 1], place)
        beta = beta_all[:, heads + h : heads + h + 1]
        couplings.append(jnp.where(strict, beta * parts[0] * gram, 0.0))
        p_ref[h] = query_key * parts[0]
        decays.append(parts[1:])
        betas.append(beta)
        rks.append(rk)
        rqs.append(rq)
    inverses = []
    pair = jnp.logical_and(strict, rows // 2 == columns // 2)
    for h in range(heads):
        inverses.append(eye_f - jnp.where(pair, couplings[h], 0.0))
    size = 2
    while size < LANES:
        band = jnp.logical_and(
            rows // (2 * size) == columns // (2 * size), rows // size > columns // size
        )
        held = [split(x) for x in inverses]
        middles = [
            mm(split(jnp.where(band, couplings[h], 0.0)), held[h]) for h in range(heads)
        ]
        inverses = [inverses[h] - mm(held[h], middles[h]) for h in range(heads)]
        size *= 2
    for h in range(heads):
        kb, qb = head_slice(k_ref, h // group), head_slice(q_ref, h // group)
        vb, dob = head_slice(v_ref, h), head_slice(do_ref, h)
        carry, to_last, last_carry = decays[h]
        beta, rk, rq = betas[h], rks[h], rqs[h]
        inverse = inverses[h]
        t_ref[h] = inverse
        w = mm(inverse * as_row(eye, beta * carry * rk), kb)
        u = mm(inverse * as_row(eye, beta), vb)
        w_out_ref[h] = w
        u_ref[h] = u
        weight = rk * to_last
        a_ref[h] = last_carry * eye_f - mm(kb, w * weight, TN)
        b_ref[h] = mm(kb, u * weight, TN)
        reach = (carry * rq) * qb.astype(f32) - mm(p_ref[h], w)
        n_ref[h] = mm(reach, dob, TN)


def chain_kernel(
    count, names, half, a_ref, b_ref, n_ref, s_ref, l_ref,
    pa, pb, pn, s_in, l_in, s_send, l_send, s_give, l_give, ca, cb, cn,
    swap_send, swap_recv, s_ss, s_rs, l_ss, l_rs, g_send, g_recv,
):
    ctx, dp = names
    me = lax.axis_index(ctx)
    core = lax.rem(me, 2)
    chip = me // 2
    chips = count // 2
    mate = me + 1 - 2 * core

    def at(place):
        return {ctx: place}

    barrier = pltpu.get_barrier_semaphore()
    pl.semaphore_signal(barrier, inc=1, device_id=at(mate), device_id_type=MESH)

    @pl.when(chip > 0)
    def _():
        pl.semaphore_signal(barrier, inc=1, device_id=at(me - 2), device_id_type=MESH)

    @pl.when(chip < chips - 1)
    def _():
        pl.semaphore_signal(barrier, inc=1, device_id=at(me + 2), device_id_type=MESH)

    around = 1 + (chip > 0).astype(jnp.int32) + (chip < chips - 1).astype(jnp.int32)
    pl.semaphore_wait(barrier, around)

    mine = core * half
    theirs = (1 - core) * half
    swaps = []
    for i, (source, target) in enumerate(((a_ref, pa), (b_ref, pb), (n_ref, pn))):
        copy = pltpu.make_async_remote_copy(
            src_ref=source.at[pl.ds(theirs, half)], dst_ref=target,
            send_sem=swap_send.at[i], recv_sem=swap_recv.at[i],
            device_id=at(mate), device_id_type=MESH,
        )
        copy.start()
        swaps.append(copy)
    for copy in swaps:
        copy.wait()

    def compose(first_a, first_b, first_n, second_a, second_b, second_n):
        for h in range(half):
            later = split(second_a(h))
            earlier = split(first_a(h))
            ca[h] = mm(later, earlier)
            cb[h] = mm(later, first_b(h)) + second_b(h)
            cn[h] = mm(earlier, second_n(h), TN) + first_n(h)

    own = [lambda h, r=r: r[mine + h] for r in (a_ref, b_ref, n_ref)]
    other = [lambda h, r=r: r[h] for r in (pa, pb, pn)]

    @pl.when(core == 0)
    def _():
        compose(*own, *other)

    @pl.when(core == 1)
    def _():
        compose(*other, *own)

    def s_copy(h):
        return pltpu.make_async_remote_copy(
            src_ref=s_send.at[h], dst_ref=s_in.at[h], send_sem=s_ss.at[h],
            recv_sem=s_rs.at[h], device_id=at(me + 2), device_id_type=MESH,
        )

    def l_copy(h):
        return pltpu.make_async_remote_copy(
            src_ref=l_send.at[h], dst_ref=l_in.at[h], send_sem=l_ss.at[h],
            recv_sem=l_rs.at[h], device_id=at(me - 2), device_id_type=MESH,
        )

    def forward():
        for h in range(half):

            @pl.when(chip == 0)
            def _():
                s_in[h] = jnp.zeros((DK, DV), f32)
                s_send[h] = cb[h]

            @pl.when(chip > 0)
            def _():
                s_copy(h).wait_recv()

                @pl.when(chip < chips - 1)
                def _():
                    s_send[h] = mm(ca[h], s_in[h]) + cb[h]

            @pl.when(chip < chips - 1)
            def _():
                s_copy(h).start()

    def backward():
        for h in range(half):

            @pl.when(chip == chips - 1)
            def _():
                l_in[h] = jnp.zeros((DK, DV), f32)
                l_send[h] = cn[h]

            @pl.when(chip < chips - 1)
            def _():
                l_copy(h).wait_recv()

                @pl.when(chip > 0)
                def _():
                    l_send[h] = mm(ca[h], l_in[h], TN) + cn[h]

            @pl.when(chip > 0)
            def _():
                l_copy(h).start()

    def give(source, target, i):
        return pltpu.make_async_remote_copy(
            src_ref=source, dst_ref=target.at[pl.ds(mine, half)], send_sem=g_send.at[i],
            recv_sem=g_recv.at[i], device_id=at(mate), device_id_type=MESH,
        )

    def finish_s():
        @pl.when(core == 0)
        def _():
            for h in range(half):
                s_ref[mine + h] = s_in[h]
                s_give[h] = mm(a_ref[mine + h], s_in[h]) + b_ref[mine + h]

        @pl.when(core == 1)
        def _():
            for h in range(half):
                s_ref[mine + h] = mm(pa[h], s_in[h]) + pb[h]
                s_give[h] = s_in[h]

        give(s_give, s_ref, 0).start()

    def finish_l():
        @pl.when(core == 1)
        def _():
            for h in range(half):
                l_ref[mine + h] = l_in[h]
                l_give[h] = mm(a_ref[mine + h], l_in[h], TN) + n_ref[mine + h]

        @pl.when(core == 0)
        def _():
            for h in range(half):
                l_ref[mine + h] = mm(pa[h], l_in[h], TN) + pn[h]
                l_give[h] = l_in[h]

        give(l_give, l_ref, 1).start()

    @pl.when(2 * chip < chips)
    def _():
        forward()
        finish_s()
        backward()
        finish_l()

    @pl.when(2 * chip >= chips)
    def _():
        backward()
        finish_l()
        forward()
        finish_s()

    for h in range(half):

        @pl.when(chip < chips - 1)
        def _():
            s_copy(h).wait_send()

        @pl.when(chip > 0)
        def _():
            l_copy(h).wait_send()

    for i, (source, target) in enumerate(((s_give, s_ref), (l_give, l_ref))):
        give(source, target, i).wait_send()
        give(source, target, i).wait_recv()


def last_kernel(
    heads, place_ref, hid_ref, q_ref, k_ref, v_ref, do_ref, rate_ref, bias_ref,
    t_ref, w_ref, u0_ref, p_ref, logit_ref, cum_ref, s_ref, l_ref,
    dq_ref, dk_ref, dv_ref, lg_ref, wg_ref, small_ref,
):
    rows, columns = iotas()
    eye = rows == columns
    lower = rows >= columns
    strict = rows > columns
    place = place_ref[0]
    logits = logit_ref[...]
    cum = cum_ref[...]
    beta_all = sigmoid(logits)
    last_row = rows[:, :1] == LANES - 1
    group = heads // (q_ref.shape[1] // DK)
    cum_grad = jnp.zeros((LANES, LANES), f32)
    beta_grad = jnp.zeros((LANES, LANES), f32)
    for h in range(heads):
        if h % group == 0:
            kb, qb = head_slice(k_ref, h // group), head_slice(q_ref, h // group)
            kf, qf = kb.astype(f32), qb.astype(f32)
            rk = scales(kb)
            rq0 = scales(qb)
            rq = rq0 * DK ** (-0.5)
            rk_row = as_row(eye, rk)
            gram = one_pass(kb, kb, NT) * rk * rk_row
            query_key = one_pass(qb, kb, NT) * rq * rk_row
            score_sum = jnp.zeros((LANES, LANES), f32)
            gram_sum = jnp.zeros((LANES, LANES), f32)
            q_hat_grad = jnp.zeros((LANES, DK), f32)
            k_hat_grad = jnp.zeros((LANES, DK), f32)
        vb, dob = head_slice(v_ref, h), head_slice(do_ref, h)
        dof = dob.astype(f32)
        decay, carry, to_last, last_carry = decay_parts(
            eye, lower, rows, columns, cum[:, h : h + 1], place
        )
        beta = beta_all[:, heads + h : heads + h + 1]
        state_f, adjoint_f = s_ref[h], l_ref[h]
        state, adjoint = split(state_f), split(adjoint_f)
        key_state = mm(kb, state) * rk
        query_state = mm(qb, state) * rq
        updates_f = u0_ref[h] - mm(w_ref[h], state)
        updates = split(updates_f)
        update_grad = mm(p_ref[h], dob, TN) + mm(kb, adjoint) * (rk * to_last)
        score_grad = mm(dob, updates, NT) * decay
        z_f = mm(t_ref[h], update_grad, TN)
        z = split(z_f)
        dv_ref[:, h * DV : (h + 1) * DV] = (beta * z_f).astype(bf16)
        coupling_grad = jnp.where(strict, -mm(z, updates, NT), 0.0) * decay
        gram_grad = coupling_grad * beta
        last_keys = mm(updates, adjoint, NT)
        q_hat_grad += carry * mm(dob, state, NT)
        k_hat_grad += last_keys * to_last - (beta * carry) * mm(z, state, NT)
        score_sum += score_grad
        gram_sum += gram_grad
        value_f = vb.astype(f32)
        along = coupling_grad * gram
        beta_col = rsum(z_f * (value_f - carry * key_state)) + rsum(along)
        carry_grad = rsum(dof * query_state) - beta * rsum(z_f * key_state)
        spread = score_grad * query_key + along * beta
        to_last_grad = rsum(last_keys * kf) * rk * to_last
        whole = jnp.sum(adjoint_f * state_f, keepdims=True) * last_carry
        whole = whole + jnp.sum(to_last_grad, axis=0, keepdims=True)
        cum_col = (
            rsum(spread)
            - as_column(eye, jnp.sum(spread, axis=0, keepdims=True))
            - to_last_grad
            + carry_grad * carry
            + jnp.where(last_row, whole, 0.0)
        )
        cum_grad = jnp.where(columns == h, cum_col, cum_grad)
        beta_grad = jnp.where(columns == heads + h, beta_col, beta_grad)
        if h % group == group - 1:
            q_hat_grad += mm(score_sum * rk_row, kb)
            k_hat_grad += (
                mm(score_sum * rq, qb, TN)
                + mm(gram_sum * rk_row, kb)
                + mm(gram_sum * rk, kb, TN)
            )
            q_dot = rsum(q_hat_grad * qf)
            k_dot = rsum(k_hat_grad * kf)
            place_q = slice((h // group) * DK, (h // group + 1) * DK)
            dq_ref[:, place_q] = (rq * (q_hat_grad - qf * (rq0 * rq0 * q_dot))).astype(bf16)
            dk_ref[:, place_q] = (rk * (k_hat_grad - kf * (rk * rk * k_dot))).astype(bf16)
    ones = lower.astype(f32).astype(bf16)
    decay_grad = mm(ones, split3(cum_grad), TN)
    log_decay = gates(logits, rate_ref[...], bias_ref[...], heads)
    x = logits + bias_ref[...]
    decay_logit = decay_grad * (-jnp.exp(rate_ref[...])) * sigmoid(x)
    logit_grad = jnp.where(
        columns < heads, decay_logit, beta_grad * beta_all * (1.0 - beta_all)
    )
    logit_grad = jnp.where(columns < 2 * heads, logit_grad, 0.0)
    lg_ref[...] = logit_grad.T[: 2 * heads, :]
    small_ref[0:1, :] = jnp.sum(decay_grad * log_decay, axis=0, keepdims=True)
    small_ref[1:2, :] = jnp.sum(decay_logit, axis=0, keepdims=True)
    wg_ref[...] = mm(split3(logit_grad), hid_ref[...], TN)[: 2 * heads, :]


def sum_kernel(
    sizes, names, x_ref, lg_ref, w_ref, sum_ref, hid_ref,
    parts, total, logits, ss, rs, ss2, rs2, lss, lrs,
):
    count, dp_count = sizes
    ctx, dp = names
    me = lax.axis_index(ctx)
    row = lax.axis_index(dp)

    barrier = pltpu.get_barrier_semaphore()

    def greet(step, _):
        peer = lax.rem(me + step, count)
        pl.semaphore_signal(barrier, inc=1, device_id={ctx: peer}, device_id_type=MESH)
        return 0

    def greet_row(step, _):
        peer = lax.rem(row + step, dp_count)
        pl.semaphore_signal(barrier, inc=1, device_id={dp: peer}, device_id_type=MESH)
        return 0

    lax.fori_loop(1, count, greet, 0)
    lax.fori_loop(1, dp_count, greet_row, 0)
    pl.semaphore_wait(barrier, count - 1 + dp_count - 1)

    def logit_copy(step):
        peer = lax.rem(row + step, dp_count)
        return pltpu.make_async_remote_copy(
            src_ref=lg_ref, dst_ref=logits.at[row], send_sem=lss.at[step],
            recv_sem=lrs.at[step], device_id={dp: peer}, device_id_type=MESH,
        )

    def scatter(step):
        peer = lax.rem(me + step, count)
        return pltpu.make_async_remote_copy(
            src_ref=x_ref.at[peer], dst_ref=parts.at[me], send_sem=ss.at[step],
            recv_sem=rs.at[step], device_id={ctx: peer}, device_id_type=MESH,
        )

    def gather(step):
        peer = lax.rem(me + step, count)
        return pltpu.make_async_remote_copy(
            src_ref=total, dst_ref=sum_ref.at[me], send_sem=ss2.at[step],
            recv_sem=rs2.at[step], device_id={ctx: peer}, device_id_type=MESH,
        )

    def each(last, act):
        def body(step, _):
            act(step)
            return 0

        lax.fori_loop(1, last, body, 0)

    each(count, lambda step: scatter(step).start())
    each(dp_count, lambda step: logit_copy(step).start())
    parts[me] = x_ref[me]
    logits[row] = lg_ref[...]
    each(count, lambda step: scatter(step).wait_recv())
    amount = parts[0]
    for i in range(1, count):
        amount = amount + parts[i]
    total[...] = amount
    sum_ref[me] = amount
    each(count, lambda step: gather(step).start())
    each(dp_count, lambda step: logit_copy(step).wait_recv())
    hidden = None
    for d in range(dp_count):
        term = mm(split3(logits[d]), w_ref[d], TN)
        hidden = term if hidden is None else hidden + term
    hid_ref[...] = hidden.astype(bf16)
    each(count, lambda step: gather(step).wait_recv())
    each(count, lambda step: scatter(step).wait_send())
    each(count, lambda step: gather(step).wait_send())
    each(dp_count, lambda step: logit_copy(step).wait_send())


def on_device(
    sizes, hidden_in, query_vectors, key_vectors, value_vectors, out_cotangent,
    w_decay, w_beta, log_decay_rate, step_bias, doc_start,
):
    count, dp_count = sizes
    tokens, width = hidden_in.shape
    heads = log_decay_rate.shape[0]
    names = ("ctx", "dp")
    vmem = pl.BlockSpec(memory_space=pltpu.VMEM)
    smem = pl.BlockSpec(memory_space=pltpu.SMEM)
    params = functools.partial(pltpu.CompilerParams, vmem_limit_bytes=VMEM_LIMIT)
    both = jnp.concatenate([w_decay, w_beta], axis=1)
    panel_w = jnp.pad(both, ((0, 0), (0, LANES - 2 * heads)))
    rate_row = jnp.pad(log_decay_rate, (0, LANES - heads))[None]
    bias_row = jnp.pad(step_bias, (0, LANES - heads))[None]
    offset = lax.axis_index("ctx") * tokens
    place = segment(doc_start, offset, tokens)
    piece = width // dp_count
    features = lax.all_gather(both.T, "dp")
    features = lax.dynamic_slice_in_dim(
        features, lax.axis_index("dp") * piece, piece, axis=2
    )

    square = jax.ShapeDtypeStruct((heads, LANES, LANES), f32)
    panel = jax.ShapeDtypeStruct((LANES, LANES), f32)
    a, b, n, t, w, u, p, logits, cum = pl.pallas_call(
        functools.partial(first_kernel, heads),
        out_shape=(square,) * 7 + (panel,) * 2,
        in_specs=[smem] + [vmem] * 8,
        out_specs=(vmem,) * 9,
        compiler_params=params(),
        name="local_maps",
    )(
        place, hidden_in, panel_w, query_vectors, key_vectors, value_vectors,
        out_cotangent, rate_row, bias_row,
    )

    half = heads // 2
    held = pltpu.VMEM((half, DK, DV), f32)
    dma = pltpu.SemaphoreType.DMA
    state, adjoint = pl.pallas_call(
        functools.partial(chain_kernel, count, names, half),
        out_shape=(square,) * 2,
        in_specs=[vmem] * 3,
        out_specs=(vmem,) * 2,
        scratch_shapes=[held] * 12
        + [dma((3,)), dma((3,))]
        + [dma((half,))] * 4
        + [dma((2,)), dma((2,))],
        compiler_params=params(collective_id=0, has_side_effects=True),
        name="chain",
    )(a, b, n)

    query_grad, key_grad, value_grad, logit_grad, weight_grad, small = pl.pallas_call(
        functools.partial(last_kernel, heads),
        out_shape=(
            jax.ShapeDtypeStruct(query_vectors.shape, bf16),
            jax.ShapeDtypeStruct(key_vectors.shape, bf16),
            jax.ShapeDtypeStruct(value_vectors.shape, bf16),
            jax.ShapeDtypeStruct((2 * heads, LANES), f32),
            jax.ShapeDtypeStruct((2 * heads, width), f32),
            jax.ShapeDtypeStruct((2, LANES), f32),
        ),
        in_specs=[smem] + [vmem] * 15,
        out_specs=(vmem,) * 6,
        compiler_params=params(),
        name="gradients",
    )(
        place, hidden_in, query_vectors, key_vectors, value_vectors, out_cotangent,
        rate_row, bias_row, t, w, u, p, logits, cum, state, adjoint,
    )

    lines = 2 * heads * width // LANES
    per = -(-lines // count)
    stacked = weight_grad.reshape(lines, LANES)
    stacked = jnp.pad(stacked, ((0, per * count - lines), (0, 0))).reshape(count, per, LANES)
    stacked = jnp.concatenate(
        [stacked, jnp.broadcast_to(small[None], (count, 2, LANES))], axis=1
    )
    summed, hidden_grad = pl.pallas_call(
        functools.partial(sum_kernel, sizes, names),
        out_shape=(
            jax.ShapeDtypeStruct(stacked.shape, f32),
            jax.ShapeDtypeStruct((tokens, piece), bf16),
        ),
        in_specs=[vmem] * 3,
        out_specs=(vmem,) * 2,
        scratch_shapes=[
            pltpu.VMEM(stacked.shape, f32),
            pltpu.VMEM(stacked.shape[1:], f32),
            pltpu.VMEM((dp_count,) + logit_grad.shape, f32),
        ]
        + [dma((count,))] * 4
        + [dma((dp_count,))] * 2,
        compiler_params=params(collective_id=1, has_side_effects=True),
        name="totals",
    )(stacked, logit_grad, features)
    weights = summed[:, :per].reshape(per * count, LANES)[:lines].reshape(2 * heads, width).T
    return (
        query_grad,
        key_grad,
        value_grad,
        hidden_grad,
        weights[:, :heads],
        weights[:, heads:],
        summed[0, per, :heads],
        summed[0, per + 1, :heads],
    )


def solution(mesh):
    in_specs = (
        P("ctx", None),
        P("ctx", "dp"),
        P("ctx", "dp"),
        P("ctx", "dp"),
        P("ctx", "dp"),
        P(None, "dp"),
        P(None, "dp"),
        P("dp"),
        P("dp"),
        P(),
    )
    out_specs = (
        P("ctx", "dp"),
        P("ctx", "dp"),
        P("ctx", "dp"),
        P("ctx", "dp"),
        P(None, "dp"),
        P(None, "dp"),
        P("dp"),
        P("dp"),
    )
    sizes = (mesh.shape["ctx"], mesh.shape["dp"])
    return jax.shard_map(
        functools.partial(on_device, sizes),
        mesh=mesh,
        in_specs=in_specs,
        out_specs=out_specs,
        check_vma=False,
    )
```

```python
import functools

import jax
import jax.numpy as jnp
from jax import lax
from jax.experimental import pallas as pl
from jax.experimental.pallas import tpu as pltpu
from jax.sharding import PartitionSpec as P

DK = 128
DV = 128
LANES = 128
norm_epsilon = 1e-06

MESH = pl.DeviceIdType.MESH
NN = ((1,), (0,))
NT = ((1,), (1,))
TN = ((0,), (0,))
f32 = jnp.float32
bf16 = jnp.bfloat16
VMEM_LIMIT = 56 * 1024 * 1024


def one_pass(a, b, dims):
    return lax.dot_general(a, b, (dims, ((), ())), preferred_element_type=f32)


def split(x):
    if isinstance(x, tuple):
        return x
    if x.dtype == bf16:
        return (x,)
    high = x.astype(bf16)
    return (high, (x - high.astype(f32)).astype(bf16))


def split3(x):
    high = x.astype(bf16)
    rest = x - high.astype(f32)
    middle = rest.astype(bf16)
    return (high, middle, (rest - middle.astype(f32)).astype(bf16))


def mm(a, b, dims=NN):
    a, b = split(a), split(b)
    total = None
    for i, left in enumerate(a):
        for j, right in enumerate(b):
            if i + j < max(len(a), len(b)):
                term = one_pass(left, right, dims)
                total = term if total is None else total + term
    return total


def iotas():
    rows = lax.broadcasted_iota(jnp.int32, (LANES, LANES), 0)
    columns = lax.broadcasted_iota(jnp.int32, (LANES, LANES), 1)
    return rows, columns


def as_row(eye, column):
    return jnp.sum(jnp.where(eye, column, 0.0), axis=0, keepdims=True)


def as_column(eye, row):
    return jnp.sum(jnp.where(eye, row, 0.0), axis=1, keepdims=True)


def rsum(x):
    return jnp.sum(x, axis=1, keepdims=True)


def gates(logits, rate_row, bias_row, heads):
    x = logits + bias_row
    softplus = jnp.maximum(x, 0.0) + jnp.log1p(jnp.exp(-jnp.abs(x)))
    return -jnp.exp(rate_row) * softplus


def sigmoid(x):
    return 1.0 / (1.0 + jnp.exp(-x))


def scales(raw):
    wide = raw.astype(f32)
    return lax.rsqrt(rsum(wide * wide) + norm_epsilon)


def head_slice(ref, index):
    return ref[:, index * 128 : (index + 1) * 128]


def segment(doc, offset, size):
    inside = jnp.logical_and(doc >= offset, doc < offset + size)
    place = jnp.where(inside, doc - offset, size)
    return place


def decay_parts(eye, lower, rows, columns, cum_col, place):
    cum_row = as_row(eye, cum_col)
    keep = jnp.logical_and(lower, (rows >= place) == (columns >= place))
    decay = jnp.where(keep, jnp.exp(jnp.where(keep, cum_col - cum_row, 0.0)), 0.0)
    places = rows[:, :1]
    carry = jnp.where(places < place, jnp.exp(cum_col), 0.0)
    last = cum_col[LANES - 1 : LANES, :]
    same = jnp.logical_or(places >= place, place >= LANES)
    to_last = jnp.where(same, jnp.exp(jnp.where(same, last - cum_col, 0.0)), 0.0)
    return decay, carry, to_last, carry[LANES - 1 : LANES, :]


def first_kernel(
    heads, place_ref, hid_ref, w_ref, q_ref, k_ref, v_ref, do_ref, rate_ref, bias_ref,
    wide_ref, a_ref, b_ref, n_ref, t_ref, w_out_ref, u_ref, p_ref, logit_ref, cum_ref,
):
    rows, columns = iotas()
    eye = rows == columns
    lower = rows >= columns
    strict = rows > columns
    place = place_ref[0]
    wide_ref[...] = jnp.zeros_like(wide_ref)
    wide_ref[0 : 2 * heads, :] = w_ref[...]
    logits = one_pass(hid_ref[...], wide_ref[...].astype(bf16), NT)
    logit_ref[...] = logits
    log_decay = gates(logits, rate_ref[...], bias_ref[...], heads)
    ones = lower.astype(f32).astype(bf16)
    cum = mm(ones, split3(log_decay))
    cum_ref[...] = cum
    beta_all = sigmoid(logits)
    eye_f = eye.astype(f32)
    group = heads // (q_ref.shape[1] // DK)
    decays, betas, rks, rqs, couplings = [], [], [], [], []
    for h in range(heads):
        if h % group == 0:
            kb, qb = head_slice(k_ref, h // group), head_slice(q_ref, h // group)
            rk = scales(kb)
            rq = scales(qb) * DK ** (-0.5)
            rk_row = as_row(eye, rk)
            gram = one_pass(kb, kb, NT) * rk * rk_row
            query_key = one_pass(qb, kb, NT) * rq * rk_row
        parts = decay_parts(eye, lower, rows, columns, cum[:, h : h + 1], place)
        beta = beta_all[:, heads + h : heads + h + 1]
        couplings.append(jnp.where(strict, beta * parts[0] * gram, 0.0))
        p_ref[h] = query_key * parts[0]
        decays.append(parts[1:])
        betas.append(beta)
        rks.append(rk)
        rqs.append(rq)
    inverses = []
    pair = jnp.logical_and(strict, rows // 2 == columns // 2)
    for h in range(heads):
        inverses.append(eye_f - jnp.where(pair, couplings[h], 0.0))
    size = 2
    while size < LANES:
        band = jnp.logical_and(
            rows // (2 * size) == columns // (2 * size), rows // size > columns // size
        )
        held = [split(x) for x in inverses]
        middles = [
            mm(split(jnp.where(band, couplings[h], 0.0)), held[h]) for h in range(heads)
        ]
        inverses = [inverses[h] - mm(held[h], middles[h]) for h in range(heads)]
        size *= 2
    for h in range(heads):
        kb, qb = head_slice(k_ref, h // group), head_slice(q_ref, h // group)
        vb, dob = head_slice(v_ref, h), head_slice(do_ref, h)
        carry, to_last, last_carry = decays[h]
        beta, rk, rq = betas[h], rks[h], rqs[h]
        inverse = inverses[h]
        t_ref[h] = inverse
        w = mm(inverse * as_row(eye, beta * carry * rk), kb)
        u = mm(inverse * as_row(eye, beta), vb)
        w_out_ref[h] = w
        u_ref[h] = u
        weight = rk * to_last
        a_ref[h] = last_carry * eye_f - mm(kb, w * weight, TN)
        b_ref[h] = mm(kb, u * weight, TN)
        reach = (carry * rq) * qb.astype(f32) - mm(p_ref[h], w)
        n_ref[h] = mm(reach, dob, TN)


def chain_kernel(
    count, names, half, a_ref, b_ref, n_ref, s_ref, l_ref,
    pa, pb, pn, s_in, l_in, s_send, l_send, s_give, l_give, ca, ca_low, cb, cn,
    swap_send, swap_recv, s_ss, s_rs, l_ss, l_rs, g_send, g_recv,
):
    ctx, dp = names
    me = lax.axis_index(ctx)
    core = lax.rem(me, 2)
    chip = me // 2
    chips = count // 2
    mate = me + 1 - 2 * core

    def at(place):
        return {ctx: place}

    mine = core * half
    theirs = (1 - core) * half
    swaps = []
    for i, (source, target) in enumerate(((a_ref, pa), (b_ref, pb), (n_ref, pn))):
        copy = pltpu.make_async_remote_copy(
            src_ref=source.at[pl.ds(theirs, half)], dst_ref=target,
            send_sem=swap_send.at[i], recv_sem=swap_recv.at[i],
            device_id=at(mate), device_id_type=MESH,
        )
        copy.start()
        swaps.append(copy)
    for copy in swaps:
        copy.wait()

    def compose(first_a, first_b, first_n, second_a, second_b, second_n):
        for h in range(half):
            later = split(second_a(h))
            earlier = split(first_a(h))
            ca[h], ca_low[h] = split(mm(later, earlier))
            cb[h] = mm(later, first_b(h)) + second_b(h)
            cn[h] = mm(earlier, second_n(h), TN) + first_n(h)

    own = [lambda h, r=r: r[mine + h] for r in (a_ref, b_ref, n_ref)]
    other = [lambda h, r=r: r[h] for r in (pa, pb, pn)]

    @pl.when(core == 0)
    def _():
        compose(*own, *other)

    @pl.when(core == 1)
    def _():
        compose(*other, *own)

    def s_copy(h):
        return pltpu.make_async_remote_copy(
            src_ref=s_send.at[h], dst_ref=s_in.at[h], send_sem=s_ss.at[h],
            recv_sem=s_rs.at[h], device_id=at(me + 2), device_id_type=MESH,
        )

    def l_copy(h):
        return pltpu.make_async_remote_copy(
            src_ref=l_send.at[h], dst_ref=l_in.at[h], send_sem=l_ss.at[h],
            recv_sem=l_rs.at[h], device_id=at(me - 2), device_id_type=MESH,
        )

    def forward():
        for h in range(half):

            @pl.when(chip == 0)
            def _():
                s_in[h] = jnp.zeros((DK, DV), f32)
                s_send[h] = cb[h]

            @pl.when(chip > 0)
            def _():
                s_copy(h).wait_recv()

                @pl.when(chip < chips - 1)
                def _():
                    s_send[h] = mm((ca[h], ca_low[h]), s_in[h]) + cb[h]

            @pl.when(chip < chips - 1)
            def _():
                s_copy(h).start()

    def backward():
        for h in range(half):

            @pl.when(chip == chips - 1)
            def _():
                l_in[h] = jnp.zeros((DK, DV), f32)
                l_send[h] = cn[h]

            @pl.when(chip < chips - 1)
            def _():
                l_copy(h).wait_recv()

                @pl.when(chip > 0)
                def _():
                    l_send[h] = mm((ca[h], ca_low[h]), l_in[h], TN) + cn[h]

            @pl.when(chip > 0)
            def _():
                l_copy(h).start()

    def give(source, target, i):
        return pltpu.make_async_remote_copy(
            src_ref=source, dst_ref=target.at[pl.ds(mine, half)], send_sem=g_send.at[i],
            recv_sem=g_recv.at[i], device_id=at(mate), device_id_type=MESH,
        )

    def finish_s():
        @pl.when(core == 0)
        def _():
            for h in range(half):
                s_ref[mine + h] = s_in[h]
                s_give[h] = mm(a_ref[mine + h], s_in[h]) + b_ref[mine + h]

        @pl.when(core == 1)
        def _():
            for h in range(half):
                s_ref[mine + h] = mm(pa[h], s_in[h]) + pb[h]
                s_give[h] = s_in[h]

        give(s_give, s_ref, 0).start()

    def finish_l():
        @pl.when(core == 1)
        def _():
            for h in range(half):
                l_ref[mine + h] = l_in[h]
                l_give[h] = mm(a_ref[mine + h], l_in[h], TN) + n_ref[mine + h]

        @pl.when(core == 0)
        def _():
            for h in range(half):
                l_ref[mine + h] = mm(pa[h], l_in[h], TN) + pn[h]
                l_give[h] = l_in[h]

        give(l_give, l_ref, 1).start()

    @pl.when(2 * chip < chips)
    def _():
        forward()
        finish_s()
        backward()
        finish_l()

    @pl.when(2 * chip >= chips)
    def _():
        backward()
        finish_l()
        forward()
        finish_s()

    for h in range(half):

        @pl.when(chip < chips - 1)
        def _():
            s_copy(h).wait_send()

        @pl.when(chip > 0)
        def _():
            l_copy(h).wait_send()

    for i, (source, target) in enumerate(((s_give, s_ref), (l_give, l_ref))):
        give(source, target, i).wait_send()
        give(source, target, i).wait_recv()


def last_kernel(
    heads, place_ref, hid_ref, q_ref, k_ref, v_ref, do_ref, rate_ref, bias_ref,
    t_ref, w_ref, u0_ref, p_ref, logit_ref, cum_ref, s_ref, l_ref,
    dq_ref, dk_ref, dv_ref, lg_ref, x_ref,
):
    rows, columns = iotas()
    eye = rows == columns
    lower = rows >= columns
    strict = rows > columns
    place = place_ref[0]
    logits = logit_ref[...]
    cum = cum_ref[...]
    beta_all = sigmoid(logits)
    last_row = rows[:, :1] == LANES - 1
    group = heads // (q_ref.shape[1] // DK)
    cum_grad = jnp.zeros((LANES, LANES), f32)
    beta_grad = jnp.zeros((LANES, LANES), f32)
    for h in range(heads):
        if h % group == 0:
            kb, qb = head_slice(k_ref, h // group), head_slice(q_ref, h // group)
            kf, qf = kb.astype(f32), qb.astype(f32)
            rk = scales(kb)
            rq0 = scales(qb)
            rq = rq0 * DK ** (-0.5)
            rk_row = as_row(eye, rk)
            gram = one_pass(kb, kb, NT) * rk * rk_row
            query_key = one_pass(qb, kb, NT) * rq * rk_row
            score_sum = jnp.zeros((LANES, LANES), f32)
            gram_sum = jnp.zeros((LANES, LANES), f32)
            q_hat_grad = jnp.zeros((LANES, DK), f32)
            k_hat_grad = jnp.zeros((LANES, DK), f32)
        vb, dob = head_slice(v_ref, h), head_slice(do_ref, h)
        dof = dob.astype(f32)
        decay, carry, to_last, last_carry = decay_parts(
            eye, lower, rows, columns, cum[:, h : h + 1], place
        )
        beta = beta_all[:, heads + h : heads + h + 1]
        state_f, adjoint_f = s_ref[h], l_ref[h]
        state, adjoint = split(state_f), split(adjoint_f)
        key_state = mm(kb, state) * rk
        query_state = mm(qb, state) * rq
        updates_f = u0_ref[h] - mm(w_ref[h], state)
        updates = split(updates_f)
        update_grad = mm(p_ref[h], dob, TN) + mm(kb, adjoint) * (rk * to_last)
        score_grad = mm(dob, updates, NT) * decay
        z_f = mm(t_ref[h], update_grad, TN)
        z = split(z_f)
        dv_ref[:, h * DV : (h + 1) * DV] = (beta * z_f).astype(bf16)
        coupling_grad = jnp.where(strict, -mm(z, updates, NT), 0.0) * decay
        gram_grad = coupling_grad * beta
        last_keys = mm(updates, adjoint, NT)
        q_hat_grad += carry * mm(dob, state, NT)
        k_hat_grad += last_keys * to_last - (beta * carry) * mm(z, state, NT)
        score_sum += score_grad
        gram_sum += gram_grad
        value_f = vb.astype(f32)
        along = coupling_grad * gram
        beta_col = rsum(z_f * (value_f - carry * key_state)) + rsum(along)
        carry_grad = rsum(dof * query_state) - beta * rsum(z_f * key_state)
        spread = score_grad * query_key + along * beta
        to_last_grad = rsum(last_keys * kf) * rk * to_last
        whole = jnp.sum(adjoint_f * state_f, keepdims=True) * last_carry
        whole = whole + jnp.sum(to_last_grad, axis=0, keepdims=True)
        cum_col = (
            rsum(spread)
            - as_column(eye, jnp.sum(spread, axis=0, keepdims=True))
            - to_last_grad
            + carry_grad * carry
            + jnp.where(last_row, whole, 0.0)
        )
        cum_grad = jnp.where(columns == h, cum_col, cum_grad)
        beta_grad = jnp.where(columns == heads + h, beta_col, beta_grad)
        if h % group == group - 1:
            q_hat_grad += mm(score_sum * rk_row, kb)
            k_hat_grad += (
                mm(score_sum * rq, qb, TN)
                + mm(gram_sum * rk_row, kb)
                + mm(gram_sum * rk, kb, TN)
            )
            q_dot = rsum(q_hat_grad * qf)
            k_dot = rsum(k_hat_grad * kf)
            place_q = slice((h // group) * DK, (h // group + 1) * DK)
            dq_ref[:, place_q] = (rq * (q_hat_grad - qf * (rq0 * rq0 * q_dot))).astype(bf16)
            dk_ref[:, place_q] = (rk * (k_hat_grad - kf * (rk * rk * k_dot))).astype(bf16)
    ones = lower.astype(f32).astype(bf16)
    decay_grad = mm(ones, split3(cum_grad), TN)
    log_decay = gates(logits, rate_ref[...], bias_ref[...], heads)
    x = logits + bias_ref[...]
    decay_logit = decay_grad * (-jnp.exp(rate_ref[...])) * sigmoid(x)
    logit_grad = jnp.where(
        columns < heads, decay_logit, beta_grad * beta_all * (1.0 - beta_all)
    )
    logit_grad = jnp.where(columns < 2 * heads, logit_grad, 0.0)
    lg_ref[...] = logit_grad.T[: 2 * heads, :]
    x_ref[0 : 2 * heads, :] = mm(split3(logit_grad), hid_ref[...], TN)[: 2 * heads, :]
    rate_grad = jnp.sum(decay_grad * log_decay, axis=0, keepdims=True)
    bias_grad = jnp.sum(decay_logit, axis=0, keepdims=True)
    for block in range(x_ref.shape[1] // LANES):
        place_x = slice(block * LANES, (block + 1) * LANES)
        x_ref[2 * heads : 2 * heads + 1, place_x] = rate_grad
        x_ref[2 * heads + 1 : 2 * heads + 2, place_x] = bias_grad


def greet_all(sizes, names):
    barrier = pltpu.get_barrier_semaphore()
    for size, name in zip(sizes, names):
        place = lax.axis_index(name)

        def greet(step, _, size=size, name=name, place=place):
            peer = lax.rem(place + step, size)
            pl.semaphore_signal(
                barrier, inc=1, device_id={name: peer}, device_id_type=MESH
            )
            return 0

        lax.fori_loop(1, size, greet, 0)
    return barrier


def each(first, last, act):
    def body(step, _):
        act(step)
        return 0

    lax.fori_loop(first, last, body, 0)


def feature_copy(sizes, names, w_ref, features, send, recv, step):
    row = lax.axis_index(names[1])
    peer = lax.rem(row + step, sizes[1])
    piece = features.shape[2]
    start = pl.multiple_of(peer * piece, LANES)
    return pltpu.make_async_remote_copy(
        src_ref=w_ref.at[:, pl.ds(start, piece)], dst_ref=features.at[row],
        send_sem=send.at[step], recv_sem=recv.at[step],
        device_id={names[1]: peer}, device_id_type=MESH,
    )


def sum_kernel(
    sizes, names, heads, x_ref, lg_ref, features, hid_ref, decay_ref, beta_ref, small_ref,
    parts, total, sums, logits, ss, rs, ss2, rs2, lss, lrs,
):
    count, dp_count = sizes
    ctx, dp = names
    me = lax.axis_index(ctx)
    row = lax.axis_index(dp)
    block = parts.shape[2]
    owners = x_ref.shape[1] // block

    def columns_of(owner):
        return pl.ds(pl.multiple_of(owner * block, LANES), block)

    def logit_copy(step):
        peer = lax.rem(row + step, dp_count)
        return pltpu.make_async_remote_copy(
            src_ref=lg_ref, dst_ref=logits.at[row], send_sem=lss.at[step],
            recv_sem=lrs.at[step], device_id={dp: peer}, device_id_type=MESH,
        )

    def scatter(step):
        owner = lax.rem(me + step, count)
        return owner, lambda: pltpu.make_async_remote_copy(
            src_ref=x_ref.at[:, columns_of(owner)], dst_ref=parts.at[me],
            send_sem=ss.at[step], recv_sem=rs.at[step],
            device_id={ctx: owner}, device_id_type=MESH,
        )

    def gather(step):
        peer = lax.rem(me + step, count)
        return pltpu.make_async_remote_copy(
            src_ref=total, dst_ref=sums.at[:, columns_of(me)], send_sem=ss2.at[step],
            recv_sem=rs2.at[step], device_id={ctx: peer}, device_id_type=MESH,
        )

    def from_owner(step):
        owner = lax.rem(me - step + count, count)
        return owner, lambda: pltpu.make_async_remote_copy(
            src_ref=total, dst_ref=sums.at[:, columns_of(owner)], send_sem=ss2.at[step],
            recv_sem=rs2.at[step], device_id={ctx: owner}, device_id_type=MESH,
        )

    def if_owner(owner, act):
        if owners == count:
            act()
        else:
            pl.when(owner < owners)(act)

    def scatter_start(step):
        owner, copy = scatter(step)
        if_owner(owner, lambda: copy().start())

    def scatter_done(step):
        owner, copy = scatter(step)
        if_owner(owner, lambda: copy().wait_send())

    def gather_done(step):
        owner, copy = from_owner(step)
        if_owner(owner, lambda: copy().wait_recv())

    each(1, count, scatter_start)
    each(1, dp_count, lambda step: logit_copy(step).start())
    logits[row] = lg_ref[...]

    def own():
        parts[me] = x_ref[:, columns_of(me)]
        each(1, count, lambda step: scatter(step)[1]().wait_recv())
        amount = parts[0]
        for i in range(1, count):
            amount = amount + parts[i]
        total[...] = amount
        sums[:, columns_of(me)] = amount
        each(1, count, lambda step: gather(step).start())

    if_owner(me, own)
    each(1, dp_count, lambda step: logit_copy(step).wait_recv())
    hidden = None
    for d in range(dp_count):
        term = mm(split3(logits[d]), features[d].astype(bf16), TN)
        hidden = term if hidden is None else hidden + term
    hid_ref[...] = hidden.astype(bf16)
    each(1, count, gather_done)
    decay_ref[...] = sums[0:heads, :]
    beta_ref[...] = sums[heads : 2 * heads, :]
    small_ref[...] = sums[2 * heads : 2 * heads + 2, 0:LANES]
    each(1, count, scatter_done)
    if_owner(me, lambda: each(1, count, lambda step: gather(step).wait_send()))
    each(1, dp_count, lambda step: logit_copy(step).wait_send())


def whole_kernel(
    sizes, names, heads, place_ref, hid_ref, w_ref, q_ref, k_ref, v_ref, do_ref, rate_ref,
    bias_ref, dq_ref, dk_ref, dv_ref, hidden_ref, decay_ref, beta_ref, small_ref,
    wide, a, b, n, t, w, u, p, s, l, logit, cum, x, lg, features, fs, fr, *rest,
):
    chain_rest, sum_rest = rest[:21], rest[21:]
    barrier = greet_all(sizes, names)
    features[lax.axis_index(names[1])] = w_ref[
        :, pl.ds(pl.multiple_of(lax.axis_index(names[1]) * features.shape[2], LANES), features.shape[2])
    ]
    first_kernel(
        heads, place_ref, hid_ref, w_ref, q_ref, k_ref, v_ref, do_ref, rate_ref, bias_ref,
        wide, a, b, n, t, w, u, p, logit, cum,
    )
    pl.semaphore_wait(barrier, sizes[0] - 1 + sizes[1] - 1)

    def feature(step):
        return feature_copy(sizes, names, w_ref, features, fs, fr, step)

    each(1, sizes[1], lambda step: feature(step).start())
    chain_kernel(sizes[0], names, heads // 2, a, b, n, s, l, *chain_rest)
    last_kernel(
        heads, place_ref, hid_ref, q_ref, k_ref, v_ref, do_ref, rate_ref, bias_ref,
        t, w, u, p, logit, cum, s, l, dq_ref, dk_ref, dv_ref, lg, x,
    )
    each(1, sizes[1], lambda step: feature(step).wait())
    sum_kernel(
        sizes, names, heads, x, lg, features, hidden_ref, decay_ref, beta_ref, small_ref,
        *sum_rest,
    )


def on_device(
    sizes, hidden_in, query_vectors, key_vectors, value_vectors, out_cotangent,
    w_decay, w_beta, log_decay_rate, step_bias, doc_start,
):
    count, dp_count = sizes
    tokens, width = hidden_in.shape
    heads = log_decay_rate.shape[0]
    names = ("ctx", "dp")
    vmem = pl.BlockSpec(memory_space=pltpu.VMEM)
    smem = pl.BlockSpec(memory_space=pltpu.SMEM)
    params = functools.partial(pltpu.CompilerParams, vmem_limit_bytes=VMEM_LIMIT)
    weights = jnp.concatenate([w_decay.T, w_beta.T], axis=0).astype(f32)
    rate_row = jnp.pad(log_decay_rate, (0, LANES - heads))[None]
    bias_row = jnp.pad(step_bias, (0, LANES - heads))[None]
    offset = lax.axis_index("ctx") * tokens
    place = segment(doc_start, offset, tokens)
    piece = width // dp_count
    half = heads // 2
    lines = -(-(2 * heads + 2) // 8) * 8
    block = width // min(count, width // LANES)

    def room(*shape, kind=f32):
        return pltpu.VMEM(shape, kind)

    square = room(heads, LANES, LANES)
    held = room(half, LANES, LANES)
    split_map = room(half, LANES, LANES, kind=bf16)
    panel = room(LANES, LANES)
    dma = pltpu.SemaphoreType.DMA
    query_grad, key_grad, value_grad, hidden_grad, decay_sum, beta_sum, small = pl.pallas_call(
        functools.partial(whole_kernel, sizes, names, heads),
        out_shape=(
            jax.ShapeDtypeStruct(query_vectors.shape, bf16),
            jax.ShapeDtypeStruct(key_vectors.shape, bf16),
            jax.ShapeDtypeStruct(value_vectors.shape, bf16),
            jax.ShapeDtypeStruct((tokens, piece), bf16),
            jax.ShapeDtypeStruct((heads, width), f32),
            jax.ShapeDtypeStruct((heads, width), f32),
            jax.ShapeDtypeStruct((2, LANES), f32),
        ),
        in_specs=[smem] + [vmem] * 8,
        out_specs=(vmem,) * 7,
        scratch_shapes=[room(LANES, width)]
        + [square] * 9
        + [panel] * 2
        + [room(lines, width), room(2 * heads, LANES), room(dp_count, 2 * heads, piece)]
        + [dma((dp_count,))] * 2
        + [held] * 9
        + [split_map] * 2
        + [held] * 2
        + [dma((3,))] * 2
        + [dma((half,))] * 4
        + [dma((2,))] * 2
        + [
            room(count, lines, block),
            room(lines, block),
            room(lines, width),
            room(dp_count, 2 * heads, LANES),
        ]
        + [dma((count,))] * 4
        + [dma((dp_count,))] * 2,
        compiler_params=params(collective_id=0, has_side_effects=True),
        name="layer_backward",
    )(
        place, hidden_in, weights, query_vectors, key_vectors, value_vectors,
        out_cotangent, rate_row, bias_row,
    )
    return (
        query_grad,
        key_grad,
        value_grad,
        hidden_grad,
        decay_sum.T,
        beta_sum.T,
        small[0, :heads],
        small[1, :heads],
    )


def solution(mesh):
    in_specs = (
        P("ctx", None),
        P("ctx", "dp"),
        P("ctx", "dp"),
        P("ctx", "dp"),
        P("ctx", "dp"),
        P(None, "dp"),
        P(None, "dp"),
        P("dp"),
        P("dp"),
        P(),
    )
    out_specs = (
        P("ctx", "dp"),
        P("ctx", "dp"),
        P("ctx", "dp"),
        P("ctx", "dp"),
        P(None, "dp"),
        P(None, "dp"),
        P("dp"),
        P("dp"),
    )
    sizes = (mesh.shape["ctx"], mesh.shape["dp"])
    return jax.shard_map(
        functools.partial(on_device, sizes),
        mesh=mesh,
        in_specs=in_specs,
        out_specs=out_specs,
        check_vma=False,
    )
```

```python
import functools

import jax
import jax.numpy as jnp
from jax import lax
from jax.experimental import pallas as pl
from jax.experimental.pallas import tpu as pltpu
from jax.sharding import PartitionSpec as P

DK = 128
DV = 128
LANES = 128
CHUNKS = 2
norm_epsilon = 1e-06

MESH = pl.DeviceIdType.MESH
NN = ((1,), (0,))
NT = ((1,), (1,))
TN = ((0,), (0,))
f32 = jnp.float32
bf16 = jnp.bfloat16
VMEM_LIMIT = 56 * 1024 * 1024


def one_pass(a, b, dims):
    return lax.dot_general(a, b, (dims, ((), ())), preferred_element_type=f32)


def split(x):
    if isinstance(x, tuple):
        return x
    if x.dtype == bf16:
        return (x,)
    high = x.astype(bf16)
    return (high, (x - high.astype(f32)).astype(bf16))


def split3(x):
    high = x.astype(bf16)
    rest = x - high.astype(f32)
    middle = rest.astype(bf16)
    return (high, middle, (rest - middle.astype(f32)).astype(bf16))


def mm(a, b, dims=NN):
    a, b = split(a), split(b)
    total = None
    for i, left in enumerate(a):
        for j, right in enumerate(b):
            if i + j < max(len(a), len(b)):
                term = one_pass(left, right, dims)
                total = term if total is None else total + term
    return total


def iotas():
    rows = lax.broadcasted_iota(jnp.int32, (LANES, LANES), 0)
    columns = lax.broadcasted_iota(jnp.int32, (LANES, LANES), 1)
    return rows, columns


def as_row(eye, column):
    return jnp.sum(jnp.where(eye, column, 0.0), axis=0, keepdims=True)


def as_column(eye, row):
    return jnp.sum(jnp.where(eye, row, 0.0), axis=1, keepdims=True)


def rsum(x):
    return jnp.sum(x, axis=1, keepdims=True)


def gates(logits, rate_row, bias_row, heads):
    x = logits + bias_row
    softplus = jnp.maximum(x, 0.0) + jnp.log1p(jnp.exp(-jnp.abs(x)))
    return -jnp.exp(rate_row) * softplus


def sigmoid(x):
    return 1.0 / (1.0 + jnp.exp(-x))


def scales(raw):
    wide = raw.astype(f32)
    return lax.rsqrt(rsum(wide * wide) + norm_epsilon)


def head_slice(ref, index):
    return ref[:, index * 128 : (index + 1) * 128]


def segment(doc, offset, size):
    inside = jnp.logical_and(doc >= offset, doc < offset + size)
    place = jnp.where(inside, doc - offset, size)
    return place


def decay_parts(eye, lower, rows, columns, cum_col, place):
    cum_row = as_row(eye, cum_col)
    keep = jnp.logical_and(lower, (rows >= place) == (columns >= place))
    decay = jnp.where(keep, jnp.exp(jnp.where(keep, cum_col - cum_row, 0.0)), 0.0)
    places = rows[:, :1]
    carry = jnp.where(places < place, jnp.exp(cum_col), 0.0)
    last = cum_col[LANES - 1 : LANES, :]
    same = jnp.logical_or(places >= place, place >= LANES)
    to_last = jnp.where(same, jnp.exp(jnp.where(same, last - cum_col, 0.0)), 0.0)
    return decay, carry, to_last, carry[LANES - 1 : LANES, :]


def first_kernel(
    heads, place, hid_ref, w_ref, q_ref, k_ref, v_ref, do_ref, rate_ref, bias_ref,
    wide_ref, a_ref, b_ref, n_ref, t_ref, w_out_ref, u_ref, p_ref, logit_ref, cum_ref,
):
    rows, columns = iotas()
    eye = rows == columns
    lower = rows >= columns
    strict = rows > columns
    wide_ref[...] = jnp.zeros_like(wide_ref)
    wide_ref[0 : 2 * heads, :] = w_ref[...]
    logits = one_pass(hid_ref[...], wide_ref[...].astype(bf16), NT)
    logit_ref[...] = logits
    log_decay = gates(logits, rate_ref[...], bias_ref[...], heads)
    ones = lower.astype(f32).astype(bf16)
    cum = mm(ones, split3(log_decay))
    cum_ref[...] = cum
    beta_all = sigmoid(logits)
    eye_f = eye.astype(f32)
    group = heads // (q_ref.shape[1] // DK)
    decays, betas, rks, rqs, couplings = [], [], [], [], []
    for h in range(heads):
        if h % group == 0:
            kb, qb = head_slice(k_ref, h // group), head_slice(q_ref, h // group)
            rk = scales(kb)
            rq = scales(qb) * DK ** (-0.5)
            rk_row = as_row(eye, rk)
            gram = one_pass(kb, kb, NT) * rk * rk_row
            query_key = one_pass(qb, kb, NT) * rq * rk_row
        parts = decay_parts(eye, lower, rows, columns, cum[:, h : h + 1], place)
        beta = beta_all[:, heads + h : heads + h + 1]
        couplings.append(jnp.where(strict, beta * parts[0] * gram, 0.0))
        p_ref[h] = query_key * parts[0]
        decays.append(parts[1:])
        betas.append(beta)
        rks.append(rk)
        rqs.append(rq)
    inverses = []
    pair = jnp.logical_and(strict, rows // 2 == columns // 2)
    for h in range(heads):
        inverses.append(eye_f - jnp.where(pair, couplings[h], 0.0))
    size = 2
    while size < LANES:
        band = jnp.logical_and(
            rows // (2 * size) == columns // (2 * size), rows // size > columns // size
        )
        held = [split(x) for x in inverses]
        middles = [
            mm(split(jnp.where(band, couplings[h], 0.0)), held[h]) for h in range(heads)
        ]
        inverses = [inverses[h] - mm(held[h], middles[h]) for h in range(heads)]
        size *= 2
    for h in range(heads):
        kb, qb = head_slice(k_ref, h // group), head_slice(q_ref, h // group)
        vb, dob = head_slice(v_ref, h), head_slice(do_ref, h)
        carry, to_last, last_carry = decays[h]
        beta, rk, rq = betas[h], rks[h], rqs[h]
        inverse = inverses[h]
        t_ref[h] = inverse
        w = mm(inverse * as_row(eye, beta * carry * rk), kb)
        u = mm(inverse * as_row(eye, beta), vb)
        w_out_ref[h] = w
        u_ref[h] = u
        weight = rk * to_last
        a_ref[h] = last_carry * eye_f - mm(kb, w * weight, TN)
        b_ref[h] = mm(u * weight, kb, TN)
        reach = (carry * rq) * qb.astype(f32) - mm(p_ref[h], w)
        n_ref[h] = mm(dob, reach, TN)


def chain_kernel(
    count, names, half, a_ref, b_ref, n_ref, s_ref, l_ref,
    pa, pb, pn, s_in, l_in, s_send, l_send, s_give, l_give, ca, ca_low, cb, cn,
    swap_send, swap_recv, s_ss, s_rs, l_ss, l_rs, gs_send, gs_recv, gl_send, gl_recv,
):
    ctx, dp = names
    me = lax.axis_index(ctx)
    core = lax.rem(me, 2)
    chip = me // 2
    chips = count // 2
    mate = me + 1 - 2 * core

    def at(place):
        return {ctx: place}

    mine = core * half
    theirs = (1 - core) * half
    swaps = []
    for i, (source, target) in enumerate(((a_ref, pa), (b_ref, pb), (n_ref, pn))):
        copy = pltpu.make_async_remote_copy(
            src_ref=source.at[pl.ds(theirs, half)], dst_ref=target,
            send_sem=swap_send.at[i], recv_sem=swap_recv.at[i],
            device_id=at(mate), device_id_type=MESH,
        )
        copy.start()
        swaps.append(copy)
    for copy in swaps:
        copy.wait()

    def compose(first_a, first_b, first_n, second_a, second_b, second_n):
        for h in range(half):
            later = split(second_a(h))
            earlier = split(first_a(h))
            ca[h], ca_low[h] = split(mm(later, earlier))
            cb[h] = mm(first_b(h), later, NT) + second_b(h)
            cn[h] = mm(second_n(h), earlier) + first_n(h)

    own = [lambda h, r=r: r[mine + h] for r in (a_ref, b_ref, n_ref)]
    other = [lambda h, r=r: r[h] for r in (pa, pb, pn)]

    @pl.when(core == 0)
    def _():
        compose(*own, *other)

    @pl.when(core == 1)
    def _():
        compose(*other, *own)

    rows = DV // CHUNKS
    units = half * CHUNKS

    def part(ref, i, head=None):
        head = i // CHUNKS if head is None else head
        return ref.at[head, pl.ds((i % CHUNKS) * rows, rows)]

    def s_copy(i):
        return pltpu.make_async_remote_copy(
            src_ref=part(s_send, i), dst_ref=part(s_in, i), send_sem=s_ss.at[i],
            recv_sem=s_rs.at[i], device_id=at(me + 2), device_id_type=MESH,
        )

    def l_copy(i):
        return pltpu.make_async_remote_copy(
            src_ref=part(l_send, i), dst_ref=part(l_in, i), send_sem=l_ss.at[i],
            recv_sem=l_rs.at[i], device_id=at(me - 2), device_id_type=MESH,
        )

    def give(source, target, i, send, recv):
        return pltpu.make_async_remote_copy(
            src_ref=part(source, i), dst_ref=part(target, i, mine + i // CHUNKS),
            send_sem=send.at[i], recv_sem=recv.at[i],
            device_id=at(mate), device_id_type=MESH,
        )

    def forward(i):
        h = i // CHUNKS

        @pl.when(chip == 0)
        def _():
            part(s_in, i)[...] = jnp.zeros((rows, DK), f32)
            part(s_send, i)[...] = part(cb, i)[...]

        @pl.when(chip > 0)
        def _():
            s_copy(i).wait_recv()

            @pl.when(chip < chips - 1)
            def _():
                step = mm(part(s_in, i)[...], (ca[h], ca_low[h]), NT)
                part(s_send, i)[...] = step + part(cb, i)[...]

        @pl.when(chip < chips - 1)
        def _():
            s_copy(i).start()

    def backward(i):
        h = i // CHUNKS

        @pl.when(chip == chips - 1)
        def _():
            part(l_in, i)[...] = jnp.zeros((rows, DK), f32)
            part(l_send, i)[...] = part(cn, i)[...]

        @pl.when(chip < chips - 1)
        def _():
            l_copy(i).wait_recv()

            @pl.when(chip > 0)
            def _():
                step = mm(part(l_in, i)[...], (ca[h], ca_low[h]))
                part(l_send, i)[...] = step + part(cn, i)[...]

        @pl.when(chip > 0)
        def _():
            l_copy(i).start()

    def finish_s(i):
        h = i // CHUNKS
        own_part = part(s_ref, i, mine + h)

        @pl.when(core == 0)
        def _():
            state = part(s_in, i)[...]
            own_part[...] = state
            step = mm(state, a_ref[mine + h], NT)
            part(s_give, i)[...] = step + part(b_ref, i, mine + h)[...]

        @pl.when(core == 1)
        def _():
            state = part(s_in, i)[...]
            own_part[...] = mm(state, pa[h], NT) + part(pb, i)[...]
            part(s_give, i)[...] = state

        give(s_give, s_ref, i, gs_send, gs_recv).start()

    def finish_l(i):
        h = i // CHUNKS
        own_part = part(l_ref, i, mine + h)

        @pl.when(core == 1)
        def _():
            adjoint = part(l_in, i)[...]
            own_part[...] = adjoint
            step = mm(adjoint, a_ref[mine + h])
            part(l_give, i)[...] = step + part(n_ref, i, mine + h)[...]

        @pl.when(core == 0)
        def _():
            adjoint = part(l_in, i)[...]
            own_part[...] = mm(adjoint, pa[h]) + part(pn, i)[...]
            part(l_give, i)[...] = adjoint

        give(l_give, l_ref, i, gl_send, gl_recv).start()

    @pl.when(2 * chip < chips)
    def _():
        for i in range(units):
            forward(i)
        for i in range(units):
            finish_s(i)
        for i in range(units):
            backward(i)
            finish_l(i)

    @pl.when(2 * chip >= chips)
    def _():
        for i in range(units):
            backward(i)
        for i in range(units):
            finish_l(i)
        for i in range(units):
            forward(i)
            finish_s(i)

    for i in range(units):

        @pl.when(chip < chips - 1)
        def _():
            s_copy(i).wait_send()

        @pl.when(chip > 0)
        def _():
            l_copy(i).wait_send()

    for i in range(units):
        give(s_give, s_ref, i, gs_send, gs_recv).wait()
        give(l_give, l_ref, i, gl_send, gl_recv).wait()


def last_kernel(
    heads, place, hid_ref, q_ref, k_ref, v_ref, do_ref, rate_ref, bias_ref,
    t_ref, w_ref, u0_ref, p_ref, logit_ref, cum_ref, s_ref, l_ref,
    dq_ref, dk_ref, dv_ref, lg_ref, x_ref,
):
    rows, columns = iotas()
    eye = rows == columns
    lower = rows >= columns
    strict = rows > columns
    logits = logit_ref[...]
    cum = cum_ref[...]
    beta_all = sigmoid(logits)
    last_row = rows[:, :1] == LANES - 1
    group = heads // (q_ref.shape[1] // DK)
    cum_grad = jnp.zeros((LANES, LANES), f32)
    beta_grad = jnp.zeros((LANES, LANES), f32)
    for h in range(heads):
        if h % group == 0:
            kb, qb = head_slice(k_ref, h // group), head_slice(q_ref, h // group)
            kf, qf = kb.astype(f32), qb.astype(f32)
            rk = scales(kb)
            rq0 = scales(qb)
            rq = rq0 * DK ** (-0.5)
            rk_row = as_row(eye, rk)
            gram = one_pass(kb, kb, NT) * rk * rk_row
            query_key = one_pass(qb, kb, NT) * rq * rk_row
            score_sum = jnp.zeros((LANES, LANES), f32)
            gram_sum = jnp.zeros((LANES, LANES), f32)
            q_hat_grad = jnp.zeros((LANES, DK), f32)
            k_hat_grad = jnp.zeros((LANES, DK), f32)
        vb, dob = head_slice(v_ref, h), head_slice(do_ref, h)
        dof = dob.astype(f32)
        decay, carry, to_last, last_carry = decay_parts(
            eye, lower, rows, columns, cum[:, h : h + 1], place
        )
        beta = beta_all[:, heads + h : heads + h + 1]
        state_f, adjoint_f = s_ref[h], l_ref[h]
        state, adjoint = split(state_f), split(adjoint_f)
        key_state = mm(kb, state, NT) * rk
        query_state = mm(qb, state, NT) * rq
        updates_f = u0_ref[h] - mm(w_ref[h], state, NT)
        updates = split(updates_f)
        update_grad = mm(p_ref[h], dob, TN) + mm(kb, adjoint, NT) * (rk * to_last)
        score_grad = mm(dob, updates, NT) * decay
        z_f = mm(t_ref[h], update_grad, TN)
        z = split(z_f)
        dv_ref[:, h * DV : (h + 1) * DV] = (beta * z_f).astype(bf16)
        coupling_grad = jnp.where(strict, -mm(z, updates, NT), 0.0) * decay
        gram_grad = coupling_grad * beta
        last_keys = mm(updates, adjoint)
        q_hat_grad += carry * mm(dob, state)
        k_hat_grad += last_keys * to_last - (beta * carry) * mm(z, state)
        score_sum += score_grad
        gram_sum += gram_grad
        value_f = vb.astype(f32)
        along = coupling_grad * gram
        beta_col = rsum(z_f * (value_f - carry * key_state)) + rsum(along)
        carry_grad = rsum(dof * query_state) - beta * rsum(z_f * key_state)
        spread = score_grad * query_key + along * beta
        to_last_grad = rsum(last_keys * kf) * rk * to_last
        whole = jnp.sum(adjoint_f * state_f, keepdims=True) * last_carry
        whole = whole + jnp.sum(to_last_grad, axis=0, keepdims=True)
        cum_col = (
            rsum(spread)
            - as_column(eye, jnp.sum(spread, axis=0, keepdims=True))
            - to_last_grad
            + carry_grad * carry
            + jnp.where(last_row, whole, 0.0)
        )
        cum_grad = jnp.where(columns == h, cum_col, cum_grad)
        beta_grad = jnp.where(columns == heads + h, beta_col, beta_grad)
        if h % group == group - 1:
            q_hat_grad += mm(score_sum * rk_row, kb)
            k_hat_grad += (
                mm(score_sum * rq, qb, TN)
                + mm(gram_sum * rk_row, kb)
                + mm(gram_sum * rk, kb, TN)
            )
            q_dot = rsum(q_hat_grad * qf)
            k_dot = rsum(k_hat_grad * kf)
            place_q = slice((h // group) * DK, (h // group + 1) * DK)
            dq_ref[:, place_q] = (rq * (q_hat_grad - qf * (rq0 * rq0 * q_dot))).astype(bf16)
            dk_ref[:, place_q] = (rk * (k_hat_grad - kf * (rk * rk * k_dot))).astype(bf16)
    ones = lower.astype(f32).astype(bf16)
    decay_grad = mm(ones, split3(cum_grad), TN)
    log_decay = gates(logits, rate_ref[...], bias_ref[...], heads)
    x = logits + bias_ref[...]
    decay_logit = decay_grad * (-jnp.exp(rate_ref[...])) * sigmoid(x)
    logit_grad = jnp.where(
        columns < heads, decay_logit, beta_grad * beta_all * (1.0 - beta_all)
    )
    logit_grad = jnp.where(columns < 2 * heads, logit_grad, 0.0)
    lg_ref[...] = logit_grad.T[: 2 * heads, :]
    x_ref[0 : 2 * heads, :] = mm(split3(logit_grad), hid_ref[...], TN)[: 2 * heads, :]
    rate_grad = jnp.sum(decay_grad * log_decay, axis=0, keepdims=True)
    bias_grad = jnp.sum(decay_logit, axis=0, keepdims=True)
    for block in range(x_ref.shape[1] // LANES):
        place_x = slice(block * LANES, (block + 1) * LANES)
        x_ref[2 * heads : 2 * heads + 1, place_x] = rate_grad
        x_ref[2 * heads + 1 : 2 * heads + 2, place_x] = bias_grad


def greet_all(sizes, names):
    barrier = pltpu.get_barrier_semaphore()
    for size, name in zip(sizes, names):
        place = lax.axis_index(name)

        def greet(step, _, size=size, name=name, place=place):
            peer = lax.rem(place + step, size)
            pl.semaphore_signal(
                barrier, inc=1, device_id={name: peer}, device_id_type=MESH
            )
            return 0

        lax.fori_loop(1, size, greet, 0)
    return barrier


def each(first, last, act):
    def body(step, _):
        act(step)
        return 0

    lax.fori_loop(first, last, body, 0)


def feature_copy(sizes, names, w_ref, features, send, recv, step):
    row = lax.axis_index(names[1])
    peer = lax.rem(row + step, sizes[1])
    piece = features.shape[2]
    start = pl.multiple_of(peer * piece, LANES)
    return pltpu.make_async_remote_copy(
        src_ref=w_ref.at[:, pl.ds(start, piece)], dst_ref=features.at[row],
        send_sem=send.at[step], recv_sem=recv.at[step],
        device_id={names[1]: peer}, device_id_type=MESH,
    )


def sum_kernel(
    sizes, names, heads, x_ref, lg_ref, features, hid_ref, decay_ref, beta_ref, small_ref,
    parts, total, sums, logits, ss, rs, ss2, rs2, lss, lrs,
):
    count, dp_count = sizes
    ctx, dp = names
    me = lax.axis_index(ctx)
    row = lax.axis_index(dp)
    block = parts.shape[2]
    owners = x_ref.shape[1] // block

    def columns_of(owner):
        return pl.ds(pl.multiple_of(owner * block, LANES), block)

    def logit_copy(step):
        peer = lax.rem(row + step, dp_count)
        return pltpu.make_async_remote_copy(
            src_ref=lg_ref, dst_ref=logits.at[row], send_sem=lss.at[step],
            recv_sem=lrs.at[step], device_id={dp: peer}, device_id_type=MESH,
        )

    def scatter(step):
        owner = lax.rem(me + step, count)
        return owner, lambda: pltpu.make_async_remote_copy(
            src_ref=x_ref.at[:, columns_of(owner)], dst_ref=parts.at[me],
            send_sem=ss.at[step], recv_sem=rs.at[step],
            device_id={ctx: owner}, device_id_type=MESH,
        )

    def gather(step):
        peer = lax.rem(me + step, count)
        return pltpu.make_async_remote_copy(
            src_ref=total, dst_ref=sums.at[:, columns_of(me)], send_sem=ss2.at[step],
            recv_sem=rs2.at[step], device_id={ctx: peer}, device_id_type=MESH,
        )

    def from_owner(step):
        owner = lax.rem(me - step + count, count)
        return owner, lambda: pltpu.make_async_remote_copy(
            src_ref=total, dst_ref=sums.at[:, columns_of(owner)], send_sem=ss2.at[step],
            recv_sem=rs2.at[step], device_id={ctx: owner}, device_id_type=MESH,
        )

    def if_owner(owner, act):
        if owners == count:
            act()
        else:
            pl.when(owner < owners)(act)

    def scatter_start(step):
        owner, copy = scatter(step)
        if_owner(owner, lambda: copy().start())

    def scatter_done(step):
        owner, copy = scatter(step)
        if_owner(owner, lambda: copy().wait_send())

    def gather_done(step):
        owner, copy = from_owner(step)
        if_owner(owner, lambda: copy().wait_recv())

    each(1, count, scatter_start)
    each(1, dp_count, lambda step: logit_copy(step).start())
    logits[row] = lg_ref[...]

    def own():
        parts[me] = x_ref[:, columns_of(me)]
        each(1, count, lambda step: scatter(step)[1]().wait_recv())
        amount = parts[0]
        for i in range(1, count):
            amount = amount + parts[i]
        total[...] = amount
        sums[:, columns_of(me)] = amount
        each(1, count, lambda step: gather(step).start())

    if_owner(me, own)
    each(1, dp_count, lambda step: logit_copy(step).wait_recv())
    hidden = None
    for d in range(dp_count):
        term = mm(split3(logits[d]), features[d].astype(bf16), TN)
        hidden = term if hidden is None else hidden + term
    hid_ref[...] = hidden.astype(bf16)
    each(1, count, gather_done)
    decay_ref[...] = sums[0:heads, :]
    beta_ref[...] = sums[heads : 2 * heads, :]
    small_ref[...] = sums[2 * heads : 2 * heads + 2, 0:LANES]
    each(1, count, scatter_done)
    if_owner(me, lambda: each(1, count, lambda step: gather(step).wait_send()))
    each(1, dp_count, lambda step: logit_copy(step).wait_send())


def whole_kernel(
    sizes, names, heads, doc_ref, rate_in, bias_in, hid_ref, wd_ref, wb_ref, q_ref, k_ref,
    v_ref, do_ref, dq_ref, dk_ref, dv_ref, hidden_ref, decay_ref, beta_ref, small_ref,
    w_ref, rate_ref, bias_ref,
    wide, a, b, n, t, w, u, p, s, l, logit, cum, x, lg, features, fs, fr, *rest,
):
    tokens = hid_ref.shape[0]
    place = segment(doc_ref[0], lax.axis_index(names[0]) * tokens, tokens)
    w_ref[0:heads, :] = wd_ref[...].astype(f32)
    w_ref[heads : 2 * heads, :] = wb_ref[...].astype(f32)
    lane = lax.broadcasted_iota(jnp.int32, (1, LANES), 1)
    rate_row = jnp.zeros((1, LANES), f32)
    bias_row = jnp.zeros((1, LANES), f32)
    for h in range(heads):
        rate_row = jnp.where(lane == h, rate_in[h], rate_row)
        bias_row = jnp.where(lane == h, bias_in[h], bias_row)
    rate_ref[...] = rate_row
    bias_ref[...] = bias_row
    chain_rest, sum_rest = rest[:23], rest[23:]
    barrier = greet_all(sizes, names)
    features[lax.axis_index(names[1])] = w_ref[
        :, pl.ds(pl.multiple_of(lax.axis_index(names[1]) * features.shape[2], LANES), features.shape[2])
    ]
    first_kernel(
        heads, place, hid_ref, w_ref, q_ref, k_ref, v_ref, do_ref, rate_ref, bias_ref,
        wide, a, b, n, t, w, u, p, logit, cum,
    )
    pl.semaphore_wait(barrier, sizes[0] - 1 + sizes[1] - 1)

    def feature(step):
        return feature_copy(sizes, names, w_ref, features, fs, fr, step)

    each(1, sizes[1], lambda step: feature(step).start())
    chain_kernel(sizes[0], names, heads // 2, a, b, n, s, l, *chain_rest)
    last_kernel(
        heads, place, hid_ref, q_ref, k_ref, v_ref, do_ref, rate_ref, bias_ref,
        t, w, u, p, logit, cum, s, l, dq_ref, dk_ref, dv_ref, lg, x,
    )
    each(1, sizes[1], lambda step: feature(step).wait())
    sum_kernel(
        sizes, names, heads, x, lg, features, hidden_ref, decay_ref, beta_ref, small_ref,
        *sum_rest,
    )


def move_kernel(heads, *refs):
    sources, small_ref, targets = refs[:6], refs[6], refs[7:13]
    rate_ref, bias_ref, sems = refs[13:]
    copies = [
        pltpu.make_async_copy(source, target, sems.at[i])
        for i, (source, target) in enumerate(zip(sources, targets))
    ]
    for copy in copies:
        copy.start()
    rate_ref[...] = small_ref[0:1, 0:heads]
    bias_ref[...] = small_ref[1:2, 0:heads]
    for copy in copies:
        copy.wait()


def on_device(
    sizes, hidden_in, query_vectors, key_vectors, value_vectors, out_cotangent,
    w_decay, w_beta, log_decay_rate, step_bias, doc_start,
):
    count, dp_count = sizes
    tokens, width = hidden_in.shape
    heads = log_decay_rate.shape[0]
    names = ("ctx", "dp")
    vmem = pl.BlockSpec(memory_space=pltpu.VMEM)
    smem = pl.BlockSpec(memory_space=pltpu.SMEM)
    params = functools.partial(pltpu.CompilerParams, vmem_limit_bytes=VMEM_LIMIT)
    piece = width // dp_count
    half = heads // 2
    lines = -(-(2 * heads + 2) // 8) * 8
    block = width // min(count, width // LANES)

    def room(*shape, kind=f32):
        return pltpu.VMEM(shape, kind)

    square = room(heads, LANES, LANES)
    held = room(half, LANES, LANES)
    split_map = room(half, LANES, LANES, kind=bf16)
    panel = room(LANES, LANES)
    dma = pltpu.SemaphoreType.DMA
    query_grad, key_grad, value_grad, hidden_grad, decay_sum, beta_sum, small = pl.pallas_call(
        functools.partial(whole_kernel, sizes, names, heads),
        out_shape=(
            jax.ShapeDtypeStruct(query_vectors.shape, bf16),
            jax.ShapeDtypeStruct(key_vectors.shape, bf16),
            jax.ShapeDtypeStruct(value_vectors.shape, bf16),
            jax.ShapeDtypeStruct((tokens, piece), bf16),
            jax.ShapeDtypeStruct((heads, width), f32),
            jax.ShapeDtypeStruct((heads, width), f32),
            jax.ShapeDtypeStruct((2, LANES), f32),
        ),
        in_specs=[smem] * 3 + [vmem] * 7,
        out_specs=(vmem,) * 7,
        scratch_shapes=[room(2 * heads, width), room(1, LANES), room(1, LANES)]
        + [room(LANES, width)]
        + [square] * 9
        + [panel] * 2
        + [room(lines, width), room(2 * heads, LANES), room(dp_count, 2 * heads, piece)]
        + [dma((dp_count,))] * 2
        + [held] * 9
        + [split_map] * 2
        + [held] * 2
        + [dma((3,))] * 2
        + [dma((half * CHUNKS,))] * 8
        + [
            room(count, lines, block),
            room(lines, block),
            room(lines, width),
            room(dp_count, 2 * heads, LANES),
        ]
        + [dma((count,))] * 4
        + [dma((dp_count,))] * 2,
        compiler_params=params(collective_id=0, has_side_effects=True),
        name="layer_backward",
    )(
        doc_start, log_decay_rate, step_bias, hidden_in, w_decay.T, w_beta.T,
        query_vectors, key_vectors, value_vectors, out_cotangent,
    )
    moved = (query_grad, key_grad, value_grad, hidden_grad, decay_sum, beta_sum)
    anywhere = pl.BlockSpec(memory_space=pl.ANY)
    row = jax.ShapeDtypeStruct((1, heads), f32)
    *moved, rate_grad, bias_grad = pl.pallas_call(
        functools.partial(move_kernel, heads),
        out_shape=tuple(jax.ShapeDtypeStruct(m.shape, m.dtype) for m in moved) + (row, row),
        in_specs=[anywhere] * 6 + [vmem],
        out_specs=(anywhere,) * 6 + (vmem,) * 2,
        scratch_shapes=[dma((6,))],
        compiler_params=params(),
        name="results",
    )(*moved, small)
    return (*moved[:4], moved[4].T, moved[5].T, rate_grad[0], bias_grad[0])


def solution(mesh):
    in_specs = (
        P("ctx", None),
        P("ctx", "dp"),
        P("ctx", "dp"),
        P("ctx", "dp"),
        P("ctx", "dp"),
        P(None, "dp"),
        P(None, "dp"),
        P("dp"),
        P("dp"),
        P(),
    )
    out_specs = (
        P("ctx", "dp"),
        P("ctx", "dp"),
        P("ctx", "dp"),
        P("ctx", "dp"),
        P(None, "dp"),
        P(None, "dp"),
        P("dp"),
        P("dp"),
    )
    sizes = (mesh.shape["ctx"], mesh.shape["dp"])
    return jax.shard_map(
        functools.partial(on_device, sizes),
        mesh=mesh,
        in_specs=in_specs,
        out_specs=out_specs,
        check_vma=False,
    )
```

```python
import functools

import jax
import jax.numpy as jnp
from jax import lax
from jax.experimental import pallas as pl
from jax.experimental.pallas import tpu as pltpu
from jax.sharding import PartitionSpec as P

DK = 128
DV = 128
LANES = 128
CHUNKS = 2
norm_epsilon = 1e-06

MESH = pl.DeviceIdType.MESH
NN = ((1,), (0,))
NT = ((1,), (1,))
TN = ((0,), (0,))
f32 = jnp.float32
bf16 = jnp.bfloat16
VMEM_LIMIT = 56 * 1024 * 1024


def one_pass(a, b, dims):
    return lax.dot_general(a, b, (dims, ((), ())), preferred_element_type=f32)


def split(x):
    if isinstance(x, tuple):
        return x
    if x.dtype == bf16:
        return (x,)
    high = x.astype(bf16)
    return (high, (x - high.astype(f32)).astype(bf16))


def split3(x):
    high = x.astype(bf16)
    rest = x - high.astype(f32)
    middle = rest.astype(bf16)
    return (high, middle, (rest - middle.astype(f32)).astype(bf16))


def mm(a, b, dims=NN):
    a, b = split(a), split(b)
    total = None
    for i, left in enumerate(a):
        for j, right in enumerate(b):
            if i + j < max(len(a), len(b)):
                term = one_pass(left, right, dims)
                total = term if total is None else total + term
    return total


def iotas():
    rows = lax.broadcasted_iota(jnp.int32, (LANES, LANES), 0)
    columns = lax.broadcasted_iota(jnp.int32, (LANES, LANES), 1)
    return rows, columns


def as_row(eye, column):
    return jnp.sum(jnp.where(eye, column, 0.0), axis=0, keepdims=True)


def as_column(eye, row):
    return jnp.sum(jnp.where(eye, row, 0.0), axis=1, keepdims=True)


def rsum(x):
    return jnp.sum(x, axis=1, keepdims=True)


def gates(logits, rate_row, bias_row, heads):
    x = logits + bias_row
    softplus = jnp.maximum(x, 0.0) + jnp.log1p(jnp.exp(-jnp.abs(x)))
    return -jnp.exp(rate_row) * softplus


def sigmoid(x):
    return 1.0 / (1.0 + jnp.exp(-x))


def scales(raw):
    wide = raw.astype(f32)
    return lax.rsqrt(rsum(wide * wide) + norm_epsilon)


def head_slice(ref, index):
    return ref[:, index * 128 : (index + 1) * 128]


def segment(doc, offset, size):
    inside = jnp.logical_and(doc >= offset, doc < offset + size)
    place = jnp.where(inside, doc - offset, size)
    return place


def decay_parts(eye, lower, rows, columns, cum_col, place):
    cum_row = as_row(eye, cum_col)
    keep = jnp.logical_and(lower, (rows >= place) == (columns >= place))
    decay = jnp.where(keep, jnp.exp(jnp.where(keep, cum_col - cum_row, 0.0)), 0.0)
    places = rows[:, :1]
    carry = jnp.where(places < place, jnp.exp(cum_col), 0.0)
    last = cum_col[LANES - 1 : LANES, :]
    same = jnp.logical_or(places >= place, place >= LANES)
    to_last = jnp.where(same, jnp.exp(jnp.where(same, last - cum_col, 0.0)), 0.0)
    return decay, carry, to_last, carry[LANES - 1 : LANES, :]


def first_kernel(
    heads, place, hid_ref, w_ref, q_ref, k_ref, v_ref, do_ref, rate_ref, bias_ref,
    wide_ref, a_ref, b_ref, n_ref, t_ref, w_out_ref, u_ref, p_ref, logit_ref, cum_ref,
):
    rows, columns = iotas()
    eye = rows == columns
    lower = rows >= columns
    strict = rows > columns
    wide_ref[...] = jnp.zeros_like(wide_ref)
    wide_ref[0 : 2 * heads, :] = w_ref[...]
    logits = one_pass(hid_ref[...], wide_ref[...].astype(bf16), NT)
    logit_ref[...] = logits
    log_decay = gates(logits, rate_ref[...], bias_ref[...], heads)
    ones = lower.astype(f32).astype(bf16)
    cum = mm(ones, split3(log_decay))
    cum_ref[...] = cum
    beta_all = sigmoid(logits)
    eye_f = eye.astype(f32)
    group = heads // (q_ref.shape[1] // DK)
    decays, betas, rks, rqs, couplings = [], [], [], [], []
    for h in range(heads):
        if h % group == 0:
            kb, qb = head_slice(k_ref, h // group), head_slice(q_ref, h // group)
            rk = scales(kb)
            rq = scales(qb) * DK ** (-0.5)
            rk_row = as_row(eye, rk)
            gram = one_pass(kb, kb, NT) * rk * rk_row
            query_key = one_pass(qb, kb, NT) * rq * rk_row
        parts = decay_parts(eye, lower, rows, columns, cum[:, h : h + 1], place)
        beta = beta_all[:, heads + h : heads + h + 1]
        couplings.append(jnp.where(strict, beta * parts[0] * gram, 0.0))
        p_ref[h] = query_key * parts[0]
        decays.append(parts[1:])
        betas.append(beta)
        rks.append(rk)
        rqs.append(rq)
    inverses = []
    pair = jnp.logical_and(strict, rows // 2 == columns // 2)
    for h in range(heads):
        inverses.append(eye_f - jnp.where(pair, couplings[h], 0.0))
    size = 2
    while size < LANES:
        band = jnp.logical_and(
            rows // (2 * size) == columns // (2 * size), rows // size > columns // size
        )
        held = [split(x) for x in inverses]
        middles = [
            mm(split(jnp.where(band, couplings[h], 0.0)), held[h]) for h in range(heads)
        ]
        inverses = [inverses[h] - mm(held[h], middles[h]) for h in range(heads)]
        size *= 2
    for h in range(heads):
        kb, qb = head_slice(k_ref, h // group), head_slice(q_ref, h // group)
        vb, dob = head_slice(v_ref, h), head_slice(do_ref, h)
        carry, to_last, last_carry = decays[h]
        beta, rk, rq = betas[h], rks[h], rqs[h]
        inverse = inverses[h]
        t_ref[h] = inverse
        w = mm(inverse * as_row(eye, beta * carry * rk), kb)
        u = mm(inverse * as_row(eye, beta), vb)
        w_out_ref[h] = w
        u_ref[h] = u
        weight = rk * to_last
        a_ref[h] = last_carry * eye_f - mm(kb, w * weight, TN)
        b_ref[h] = mm(u * weight, kb, TN)
        reach = (carry * rq) * qb.astype(f32) - mm(p_ref[h], w)
        n_ref[h] = mm(dob, reach, TN)


def chain_kernel(
    count, names, half, a_ref, b_ref, n_ref, s_ref, l_ref,
    pa, pb, pn, s_in, l_in, s_send, l_send, s_give, l_give, ca, ca_low, cb, cn,
    swap_send, swap_recv, s_ss, s_rs, l_ss, l_rs, gs_send, gs_recv, gl_send, gl_recv,
):
    ctx, dp = names
    me = lax.axis_index(ctx)
    core = lax.rem(me, 2)
    chip = me // 2
    chips = count // 2
    mate = me + 1 - 2 * core

    def at(place):
        return {ctx: place}

    mine = core * half
    theirs = (1 - core) * half
    swaps = []
    for i, (source, target) in enumerate(((a_ref, pa), (b_ref, pb), (n_ref, pn))):
        copy = pltpu.make_async_remote_copy(
            src_ref=source.at[pl.ds(theirs, half)], dst_ref=target,
            send_sem=swap_send.at[i], recv_sem=swap_recv.at[i],
            device_id=at(mate), device_id_type=MESH,
        )
        copy.start()
        swaps.append(copy)
    for copy in swaps:
        copy.wait()

    def compose(first_a, first_b, first_n, second_a, second_b, second_n):
        for h in range(half):
            later = split(second_a(h))
            earlier = split(first_a(h))
            ca[h], ca_low[h] = split(mm(later, earlier))
            cb[h] = mm(first_b(h), later, NT) + second_b(h)
            cn[h] = mm(second_n(h), earlier) + first_n(h)

    own = [lambda h, r=r: r[mine + h] for r in (a_ref, b_ref, n_ref)]
    other = [lambda h, r=r: r[h] for r in (pa, pb, pn)]

    @pl.when(core == 0)
    def _():
        compose(*own, *other)

    @pl.when(core == 1)
    def _():
        compose(*other, *own)

    rows = DV // CHUNKS
    units = half * CHUNKS

    def part(ref, i, head=None):
        head = i // CHUNKS if head is None else head
        return ref.at[head, pl.ds((i % CHUNKS) * rows, rows)]

    def s_copy(i):
        return pltpu.make_async_remote_copy(
            src_ref=part(s_send, i), dst_ref=part(s_in, i), send_sem=s_ss.at[i],
            recv_sem=s_rs.at[i], device_id=at(me + 2), device_id_type=MESH,
        )

    def l_copy(i):
        return pltpu.make_async_remote_copy(
            src_ref=part(l_send, i), dst_ref=part(l_in, i), send_sem=l_ss.at[i],
            recv_sem=l_rs.at[i], device_id=at(me - 2), device_id_type=MESH,
        )

    def give(source, target, i, send, recv):
        return pltpu.make_async_remote_copy(
            src_ref=part(source, i), dst_ref=part(target, i, mine + i // CHUNKS),
            send_sem=send.at[i], recv_sem=recv.at[i],
            device_id=at(mate), device_id_type=MESH,
        )

    def forward(i):
        h = i // CHUNKS

        @pl.when(chip == 0)
        def _():
            part(s_in, i)[...] = jnp.zeros((rows, DK), f32)
            part(s_send, i)[...] = part(cb, i)[...]

        @pl.when(chip > 0)
        def _():
            s_copy(i).wait_recv()

            @pl.when(chip < chips - 1)
            def _():
                step = mm(part(s_in, i)[...], (ca[h], ca_low[h]), NT)
                part(s_send, i)[...] = step + part(cb, i)[...]

        @pl.when(chip < chips - 1)
        def _():
            s_copy(i).start()

    def backward(i):
        h = i // CHUNKS

        @pl.when(chip == chips - 1)
        def _():
            part(l_in, i)[...] = jnp.zeros((rows, DK), f32)
            part(l_send, i)[...] = part(cn, i)[...]

        @pl.when(chip < chips - 1)
        def _():
            l_copy(i).wait_recv()

            @pl.when(chip > 0)
            def _():
                step = mm(part(l_in, i)[...], (ca[h], ca_low[h]))
                part(l_send, i)[...] = step + part(cn, i)[...]

        @pl.when(chip > 0)
        def _():
            l_copy(i).start()

    def finish_s(i):
        h = i // CHUNKS
        own_part = part(s_ref, i, mine + h)

        @pl.when(core == 0)
        def _():
            state = part(s_in, i)[...]
            own_part[...] = state
            step = mm(state, a_ref[mine + h], NT)
            part(s_give, i)[...] = step + part(b_ref, i, mine + h)[...]

        @pl.when(core == 1)
        def _():
            state = part(s_in, i)[...]
            own_part[...] = mm(state, pa[h], NT) + part(pb, i)[...]
            part(s_give, i)[...] = state

        give(s_give, s_ref, i, gs_send, gs_recv).start()

    def finish_l(i):
        h = i // CHUNKS
        own_part = part(l_ref, i, mine + h)

        @pl.when(core == 1)
        def _():
            adjoint = part(l_in, i)[...]
            own_part[...] = adjoint
            step = mm(adjoint, a_ref[mine + h])
            part(l_give, i)[...] = step + part(n_ref, i, mine + h)[...]

        @pl.when(core == 0)
        def _():
            adjoint = part(l_in, i)[...]
            own_part[...] = mm(adjoint, pa[h]) + part(pn, i)[...]
            part(l_give, i)[...] = adjoint

        give(l_give, l_ref, i, gl_send, gl_recv).start()

    @pl.when(2 * chip < chips)
    def _():
        for i in range(units):
            forward(i)
        for i in range(units):
            finish_s(i)
        for i in range(units):
            backward(i)
            finish_l(i)

    @pl.when(2 * chip >= chips)
    def _():
        for i in range(units):
            backward(i)
        for i in range(units):
            finish_l(i)
        for i in range(units):
            forward(i)
            finish_s(i)

    for i in range(units):

        @pl.when(chip < chips - 1)
        def _():
            s_copy(i).wait_send()

        @pl.when(chip > 0)
        def _():
            l_copy(i).wait_send()

    for i in range(units):
        give(s_give, s_ref, i, gs_send, gs_recv).wait()
        give(l_give, l_ref, i, gl_send, gl_recv).wait()


def last_kernel(
    heads, place, hid_ref, q_ref, k_ref, v_ref, do_ref, rate_ref, bias_ref,
    t_ref, w_ref, u0_ref, p_ref, logit_ref, cum_ref, s_ref, l_ref,
    dq_ref, dk_ref, dv_ref, lg_ref, x_ref,
):
    rows, columns = iotas()
    eye = rows == columns
    lower = rows >= columns
    strict = rows > columns
    logits = logit_ref[...]
    cum = cum_ref[...]
    beta_all = sigmoid(logits)
    last_row = rows[:, :1] == LANES - 1
    group = heads // (q_ref.shape[1] // DK)
    cum_grad = jnp.zeros((LANES, LANES), f32)
    beta_grad = jnp.zeros((LANES, LANES), f32)
    for h in range(heads):
        if h % group == 0:
            kb, qb = head_slice(k_ref, h // group), head_slice(q_ref, h // group)
            kf, qf = kb.astype(f32), qb.astype(f32)
            rk = scales(kb)
            rq0 = scales(qb)
            rq = rq0 * DK ** (-0.5)
            rk_row = as_row(eye, rk)
            gram = one_pass(kb, kb, NT) * rk * rk_row
            query_key = one_pass(qb, kb, NT) * rq * rk_row
            score_sum = jnp.zeros((LANES, LANES), f32)
            gram_sum = jnp.zeros((LANES, LANES), f32)
            q_hat_grad = jnp.zeros((LANES, DK), f32)
            k_hat_grad = jnp.zeros((LANES, DK), f32)
        vb, dob = head_slice(v_ref, h), head_slice(do_ref, h)
        dof = dob.astype(f32)
        decay, carry, to_last, last_carry = decay_parts(
            eye, lower, rows, columns, cum[:, h : h + 1], place
        )
        beta = beta_all[:, heads + h : heads + h + 1]
        state_f, adjoint_f = s_ref[h], l_ref[h]
        state, adjoint = split(state_f), split(adjoint_f)
        key_state = mm(kb, state, NT) * rk
        query_state = mm(qb, state, NT) * rq
        updates_f = u0_ref[h] - mm(w_ref[h], state, NT)
        updates = split(updates_f)
        update_grad = mm(p_ref[h], dob, TN) + mm(kb, adjoint, NT) * (rk * to_last)
        score_grad = mm(dob, updates, NT) * decay
        z_f = mm(t_ref[h], update_grad, TN)
        z = split(z_f)
        dv_ref[:, h * DV : (h + 1) * DV] = (beta * z_f).astype(bf16)
        coupling_grad = jnp.where(strict, -mm(z, updates, NT), 0.0) * decay
        gram_grad = coupling_grad * beta
        last_keys = mm(updates, adjoint)
        q_hat_grad += carry * mm(dob, state)
        k_hat_grad += last_keys * to_last - (beta * carry) * mm(z, state)
        score_sum += score_grad
        gram_sum += gram_grad
        value_f = vb.astype(f32)
        along = coupling_grad * gram
        beta_col = rsum(z_f * (value_f - carry * key_state)) + rsum(along)
        carry_grad = rsum(dof * query_state) - beta * rsum(z_f * key_state)
        spread = score_grad * query_key + along * beta
        to_last_grad = rsum(last_keys * kf) * rk * to_last
        whole = jnp.sum(adjoint_f * state_f, keepdims=True) * last_carry
        whole = whole + jnp.sum(to_last_grad, axis=0, keepdims=True)
        cum_col = (
            rsum(spread)
            - as_column(eye, jnp.sum(spread, axis=0, keepdims=True))
            - to_last_grad
            + carry_grad * carry
            + jnp.where(last_row, whole, 0.0)
        )
        cum_grad = jnp.where(columns == h, cum_col, cum_grad)
        beta_grad = jnp.where(columns == heads + h, beta_col, beta_grad)
        if h % group == group - 1:
            q_hat_grad += mm(score_sum * rk_row, kb)
            k_hat_grad += (
                mm(score_sum * rq, qb, TN)
                + mm(gram_sum * rk_row, kb)
                + mm(gram_sum * rk, kb, TN)
            )
            q_dot = rsum(q_hat_grad * qf)
            k_dot = rsum(k_hat_grad * kf)
            place_q = slice((h // group) * DK, (h // group + 1) * DK)
            dq_ref[:, place_q] = (rq * (q_hat_grad - qf * (rq0 * rq0 * q_dot))).astype(bf16)
            dk_ref[:, place_q] = (rk * (k_hat_grad - kf * (rk * rk * k_dot))).astype(bf16)
    ones = lower.astype(f32).astype(bf16)
    decay_grad = mm(ones, split3(cum_grad), TN)
    log_decay = gates(logits, rate_ref[...], bias_ref[...], heads)
    x = logits + bias_ref[...]
    decay_logit = decay_grad * (-jnp.exp(rate_ref[...])) * sigmoid(x)
    logit_grad = jnp.where(
        columns < heads, decay_logit, beta_grad * beta_all * (1.0 - beta_all)
    )
    logit_grad = jnp.where(columns < 2 * heads, logit_grad, 0.0)
    lg_ref[...] = logit_grad.T[: 2 * heads, :]
    x_ref[0 : 2 * heads, :] = mm(split3(logit_grad), hid_ref[...], TN)[: 2 * heads, :]
    rate_grad = jnp.sum(decay_grad * log_decay, axis=0, keepdims=True)
    bias_grad = jnp.sum(decay_logit, axis=0, keepdims=True)
    for block in range(x_ref.shape[1] // LANES):
        place_x = slice(block * LANES, (block + 1) * LANES)
        x_ref[2 * heads : 2 * heads + 1, place_x] = rate_grad
        x_ref[2 * heads + 1 : 2 * heads + 2, place_x] = bias_grad


def greet_all(sizes, names):
    barrier = pltpu.get_barrier_semaphore()
    for size, name in zip(sizes, names):
        place = lax.axis_index(name)

        def greet(step, _, size=size, name=name, place=place):
            peer = lax.rem(place + step, size)
            pl.semaphore_signal(
                barrier, inc=1, device_id={name: peer}, device_id_type=MESH
            )
            return 0

        lax.fori_loop(1, size, greet, 0)
    return barrier


def each(first, last, act):
    def body(step, _):
        act(step)
        return 0

    lax.fori_loop(first, last, body, 0)


def feature_copy(sizes, names, w_ref, features, send, recv, step):
    row = lax.axis_index(names[1])
    peer = lax.rem(row + step, sizes[1])
    piece = features.shape[2]
    start = pl.multiple_of(peer * piece, LANES)
    return pltpu.make_async_remote_copy(
        src_ref=w_ref.at[:, pl.ds(start, piece)], dst_ref=features.at[row],
        send_sem=send.at[step], recv_sem=recv.at[step],
        device_id={names[1]: peer}, device_id_type=MESH,
    )


def sum_kernel(
    sizes, names, heads, x_ref, lg_ref, features, hid_ref, decay_ref, beta_ref, small_ref,
    parts, total, sums, logits, ss, rs, ss2, rs2, lss, lrs,
):
    count, dp_count = sizes
    ctx, dp = names
    me = lax.axis_index(ctx)
    row = lax.axis_index(dp)
    block = parts.shape[2]
    owners = x_ref.shape[1] // block

    def columns_of(owner):
        return pl.ds(pl.multiple_of(owner * block, LANES), block)

    def logit_copy(step):
        peer = lax.rem(row + step, dp_count)
        return pltpu.make_async_remote_copy(
            src_ref=lg_ref, dst_ref=logits.at[row], send_sem=lss.at[step],
            recv_sem=lrs.at[step], device_id={dp: peer}, device_id_type=MESH,
        )

    def scatter(step):
        owner = lax.rem(me + step, count)
        return owner, lambda: pltpu.make_async_remote_copy(
            src_ref=x_ref.at[:, columns_of(owner)], dst_ref=parts.at[me],
            send_sem=ss.at[step], recv_sem=rs.at[step],
            device_id={ctx: owner}, device_id_type=MESH,
        )

    def gather(step):
        peer = lax.rem(me + step, count)
        return pltpu.make_async_remote_copy(
            src_ref=total, dst_ref=sums.at[:, columns_of(me)], send_sem=ss2.at[step],
            recv_sem=rs2.at[step], device_id={ctx: peer}, device_id_type=MESH,
        )

    def from_owner(step):
        owner = lax.rem(me - step + count, count)
        return owner, lambda: pltpu.make_async_remote_copy(
            src_ref=total, dst_ref=sums.at[:, columns_of(owner)], send_sem=ss2.at[step],
            recv_sem=rs2.at[step], device_id={ctx: owner}, device_id_type=MESH,
        )

    def if_owner(owner, act):
        if owners == count:
            act()
        else:
            pl.when(owner < owners)(act)

    def scatter_start(step):
        owner, copy = scatter(step)
        if_owner(owner, lambda: copy().start())

    def scatter_done(step):
        owner, copy = scatter(step)
        if_owner(owner, lambda: copy().wait_send())

    def gather_done(step):
        owner, copy = from_owner(step)
        if_owner(owner, lambda: copy().wait_recv())

    each(1, count, scatter_start)
    each(1, dp_count, lambda step: logit_copy(step).start())
    logits[row] = lg_ref[...]

    def own():
        parts[me] = x_ref[:, columns_of(me)]
        each(1, count, lambda step: scatter(step)[1]().wait_recv())
        amount = parts[0]
        for i in range(1, count):
            amount = amount + parts[i]
        total[...] = amount
        sums[:, columns_of(me)] = amount
        each(1, count, lambda step: gather(step).start())

    if_owner(me, own)
    each(1, dp_count, lambda step: logit_copy(step).wait_recv())
    hidden = None
    for d in range(dp_count):
        term = mm(split3(logits[d]), features[d].astype(bf16), TN)
        hidden = term if hidden is None else hidden + term
    hid_ref[...] = hidden.astype(bf16)
    each(1, count, gather_done)
    decay_ref[...] = sums[0:heads, :]
    beta_ref[...] = sums[heads : 2 * heads, :]
    small_ref[...] = sums[2 * heads : 2 * heads + 2, 0:LANES]
    each(1, count, scatter_done)
    if_owner(me, lambda: each(1, count, lambda step: gather(step).wait_send()))
    each(1, dp_count, lambda step: logit_copy(step).wait_send())


def whole_kernel(
    sizes, names, heads, doc_ref, rate_in, bias_in, hid_ref, wd_ref, wb_ref, q_ref, k_ref,
    v_ref, do_ref, dq_ref, dk_ref, dv_ref, hidden_ref, decay_ref, beta_ref, small_ref,
    w_ref, rate_ref, bias_ref,
    wide, a, b, n, t, w, u, p, s, l, logit, cum, x, lg, features, fs, fr, *rest,
):
    tokens = hid_ref.shape[0]
    place = segment(doc_ref[0], lax.axis_index(names[0]) * tokens, tokens)
    w_ref[0:heads, :] = wd_ref[...].astype(f32)
    w_ref[heads : 2 * heads, :] = wb_ref[...].astype(f32)
    lane = lax.broadcasted_iota(jnp.int32, (1, LANES), 1)
    rate_row = jnp.zeros((1, LANES), f32)
    bias_row = jnp.zeros((1, LANES), f32)
    for h in range(heads):
        rate_row = jnp.where(lane == h, rate_in[h], rate_row)
        bias_row = jnp.where(lane == h, bias_in[h], bias_row)
    rate_ref[...] = rate_row
    bias_ref[...] = bias_row
    chain_rest, sum_rest = rest[:23], rest[23:]
    barrier = greet_all(sizes, names)
    features[lax.axis_index(names[1])] = w_ref[
        :, pl.ds(pl.multiple_of(lax.axis_index(names[1]) * features.shape[2], LANES), features.shape[2])
    ]
    first_kernel(
        heads, place, hid_ref, w_ref, q_ref, k_ref, v_ref, do_ref, rate_ref, bias_ref,
        wide, a, b, n, t, w, u, p, logit, cum,
    )
    pl.semaphore_wait(barrier, sizes[0] - 1 + sizes[1] - 1)

    def feature(step):
        return feature_copy(sizes, names, w_ref, features, fs, fr, step)

    each(1, sizes[1], lambda step: feature(step).start())
    chain_kernel(sizes[0], names, heads // 2, a, b, n, s, l, *chain_rest)
    last_kernel(
        heads, place, hid_ref, q_ref, k_ref, v_ref, do_ref, rate_ref, bias_ref,
        t, w, u, p, logit, cum, s, l, dq_ref, dk_ref, dv_ref, lg, x,
    )
    each(1, sizes[1], lambda step: feature(step).wait())
    sum_kernel(
        sizes, names, heads, x, lg, features, hidden_ref, decay_ref, beta_ref, small_ref,
        *sum_rest,
    )


def move_kernel(heads, *refs):
    sources, small_ref, targets = refs[:6], refs[6], refs[7:13]
    rate_ref, bias_ref = refs[13:]
    for source, target in zip(sources, targets):
        target[...] = source[...]
    rate_ref[...] = small_ref[0:1, 0:heads]
    bias_ref[...] = small_ref[1:2, 0:heads]


def on_device(
    sizes, hidden_in, query_vectors, key_vectors, value_vectors, out_cotangent,
    w_decay, w_beta, log_decay_rate, step_bias, doc_start,
):
    count, dp_count = sizes
    tokens, width = hidden_in.shape
    heads = log_decay_rate.shape[0]
    names = ("ctx", "dp")
    vmem = pl.BlockSpec(memory_space=pltpu.VMEM)
    smem = pl.BlockSpec(memory_space=pltpu.SMEM)
    params = functools.partial(pltpu.CompilerParams, vmem_limit_bytes=VMEM_LIMIT)
    piece = width // dp_count
    half = heads // 2
    lines = -(-(2 * heads + 2) // 8) * 8
    block = width // min(count, width // LANES)

    def room(*shape, kind=f32):
        return pltpu.VMEM(shape, kind)

    square = room(heads, LANES, LANES)
    held = room(half, LANES, LANES)
    split_map = room(half, LANES, LANES, kind=bf16)
    panel = room(LANES, LANES)
    dma = pltpu.SemaphoreType.DMA
    query_grad, key_grad, value_grad, hidden_grad, decay_sum, beta_sum, small = pl.pallas_call(
        functools.partial(whole_kernel, sizes, names, heads),
        out_shape=(
            jax.ShapeDtypeStruct(query_vectors.shape, bf16),
            jax.ShapeDtypeStruct(key_vectors.shape, bf16),
            jax.ShapeDtypeStruct(value_vectors.shape, bf16),
            jax.ShapeDtypeStruct((tokens, piece), bf16),
            jax.ShapeDtypeStruct((heads, width), f32),
            jax.ShapeDtypeStruct((heads, width), f32),
            jax.ShapeDtypeStruct((2, LANES), f32),
        ),
        in_specs=[smem] * 3 + [vmem] * 7,
        out_specs=(vmem,) * 7,
        scratch_shapes=[room(2 * heads, width), room(1, LANES), room(1, LANES)]
        + [room(LANES, width)]
        + [square] * 9
        + [panel] * 2
        + [room(lines, width), room(2 * heads, LANES), room(dp_count, 2 * heads, piece)]
        + [dma((dp_count,))] * 2
        + [held] * 9
        + [split_map] * 2
        + [held] * 2
        + [dma((3,))] * 2
        + [dma((half * CHUNKS,))] * 8
        + [
            room(count, lines, block),
            room(lines, block),
            room(lines, width),
            room(dp_count, 2 * heads, LANES),
        ]
        + [dma((count,))] * 4
        + [dma((dp_count,))] * 2,
        compiler_params=params(collective_id=0, has_side_effects=True),
        name="layer_backward",
    )(
        doc_start, log_decay_rate, step_bias, hidden_in, w_decay.T, w_beta.T,
        query_vectors, key_vectors, value_vectors, out_cotangent,
    )
    moved = (query_grad, key_grad, value_grad, hidden_grad, decay_sum, beta_sum)
    row = jax.ShapeDtypeStruct((1, heads), f32)
    *moved, rate_grad, bias_grad = pl.pallas_call(
        functools.partial(move_kernel, heads),
        out_shape=tuple(jax.ShapeDtypeStruct(m.shape, m.dtype) for m in moved) + (row, row),
        in_specs=[vmem] * 7,
        out_specs=(vmem,) * 8,
        compiler_params=params(),
        name="results",
    )(*moved, small)
    return (*moved[:4], moved[4].T, moved[5].T, rate_grad[0], bias_grad[0])


def solution(mesh):
    in_specs = (
        P("ctx", None),
        P("ctx", "dp"),
        P("ctx", "dp"),
        P("ctx", "dp"),
        P("ctx", "dp"),
        P(None, "dp"),
        P(None, "dp"),
        P("dp"),
        P("dp"),
        P(),
    )
    out_specs = (
        P("ctx", "dp"),
        P("ctx", "dp"),
        P("ctx", "dp"),
        P("ctx", "dp"),
        P(None, "dp"),
        P(None, "dp"),
        P("dp"),
        P("dp"),
    )
    sizes = (mesh.shape["ctx"], mesh.shape["dp"])
    return jax.shard_map(
        functools.partial(on_device, sizes),
        mesh=mesh,
        in_specs=in_specs,
        out_specs=out_specs,
        check_vma=False,
    )
```
